128 devices in a mesh: rep: 4 (over x), fsdp: 32 (over y, z, core).
Axes of the slice: x: 4, y: 4, z: 4, core: 2. Of those that a mesh axis runs over, the one named last changes fastest.
Arguments:
- tokens: bfloat16 [131072, 8192], P(('rep', 'fsdp')), may hold values from -6 to 6
- weight: bfloat16 [8192, 1024], P('fsdp'), may hold values from -0.0625 to 0.0625
- momentum: float32 [4, 8192, 1024], P('rep', 'fsdp'), may hold values from -6 to 6
- grad: float32 [4, 8192, 1024], P('rep', 'fsdp'), may hold values from -6 to 6
- selection: int32 [4, 128, 16, 64], replicated, may hold values from 0 to 4095, as said below
Outputs:
- keys: bfloat16 [131072, 1024], P(('rep', 'fsdp'))
- new_weight: bfloat16 [8192, 1024], P('fsdp')
- new_momentum: float32 [4, 8192, 1024], P('rep', 'fsdp')
The draws below stay inside these ranges and needn't reach their ends.
Inputs may be any that keep to these rules, and one draw needn't show every extreme that they name: `selection`: within each replica's block the 64 indices are distinct.
All inputs are finite; a program needn't handle non-finite values.
Results may differ from the reference program's by a relative error of at most 0.0049.
Values may be sent and summed in bfloat16 or wider, within the bound.
No kernel may reach another device: no remote copies, remote signals or barrier semaphores. Data moves between devices by JAX's collectives and lax.ppermute only.
A program may use at most 384 MiB of HBM per device.

```python
import jax
import jax.numpy as jnp
from jax import lax

D = 8192
KV = 1024
GROUP = 64
KEEP = 64
TOKENS = 131072
N_REP = 4


def draw_selection(key, part):
    key = jax.random.fold_in(key, 11)
    count = N_REP * (D // GROUP) * (KV // GROUP)
    subkeys = jax.random.split(key, count)
    picks = jax.vmap(lambda one: jax.random.permutation(one, GROUP * GROUP)[:KEEP])(subkeys)
    return picks.reshape(N_REP, D // GROUP, KV // GROUP, KEEP).astype(jnp.int32)


def level_of(key, shape, shards, low, high):
    gain, own = 1.0, jax.random.fold_in(key, 6)
    for position, parts in shards:
        draws = jnp.exp(jax.random.uniform(jax.random.fold_in(own, position), (parts,), jnp.float32, low / len(shards), high / len(shards)))
        gain = gain * jnp.repeat(draws, shape[position] // parts).reshape([-1 if axis == position else 1 for axis in range(len(shape))])
    return gain


def scatter_about(stream_key, extent, spread, bound, cuts=(), held_as=jnp.bfloat16):
    level = level_of(stream_key, extent, cuts, -0.22, 0.18) if cuts else 1.0
    values = jax.random.normal(stream_key, extent, jnp.float32) * spread * level
    return jnp.minimum(jnp.maximum(values, -bound), bound).astype(held_as)


def setup_inputs(seed: int = 0) -> dict:
    streams_of = jax.random.split(jax.random.key(seed), 6)
    tokens = scatter_about(streams_of[0], (TOKENS, D), 1.0, 6.0, ((0, 128),))
    weight = scatter_about(streams_of[1], (D, KV), D ** -0.5, 0.0625, ((0, 32),))
    momentum = scatter_about(streams_of[2], (N_REP, D, KV), 1.0, 6.0, ((0, 4), (1, 32)), jnp.float32)
    grad = scatter_about(streams_of[3], (N_REP, D, KV), 1.0, 6.0, ((0, 4), (1, 32)), jnp.float32)
    selection = draw_selection(jax.random.fold_in(streams_of[5], 71), 0)
    return dict(tokens=tokens, weight=weight, momentum=momentum, grad=grad, selection=selection)


beta_decay = 0.999
step_rate = 0.05

def dct_matrix():
    freq = jnp.arange(GROUP, dtype=jnp.float32)[:, None]
    place = jnp.arange(GROUP, dtype=jnp.float32)[None, :]
    scale = jnp.where(freq == 0, jnp.sqrt(1.0 / GROUP), jnp.sqrt(2.0 / GROUP))
    return (scale * jnp.cos(jnp.pi * (2.0 * place + 1.0) * freq / (2.0 * GROUP))).astype(jnp.float32)

def to_groups(matrix):
    rows, cols = matrix.shape
    return matrix.reshape(rows // GROUP, GROUP, cols // GROUP, GROUP).transpose(0, 2, 1, 3)

def from_groups(blocks):
    nrow, ncol = (blocks.shape[0], blocks.shape[1])
    return blocks.transpose(0, 2, 1, 3).reshape(nrow * GROUP, ncol * GROUP)

def forward_dct(blocks, basis):
    inner = jnp.einsum('ij,abjk->abik', basis, blocks, precision=lax.Precision.HIGHEST)
    return jnp.einsum('abik,lk->abil', inner, basis, precision=lax.Precision.HIGHEST)

def inverse_dct(blocks, basis):
    inner = jnp.einsum('ji,abjk->abik', basis, blocks, precision=lax.Precision.HIGHEST)
    return jnp.einsum('abik,kl->abil', inner, basis, precision=lax.Precision.HIGHEST)

def scatter_dense(indices, values):
    lead = indices.shape[:-1]
    width = indices.shape[-1]
    flat_idx = indices.reshape(-1, width).astype(jnp.int32)
    flat_val = values.reshape(-1, width)
    count = flat_idx.shape[0]
    rows_all = jnp.arange(count, dtype=jnp.int32)[:, None]
    dense = jnp.zeros((count, GROUP * GROUP), jnp.float32).at[rows_all, flat_idx].add(flat_val)
    return dense.reshape(lead + (GROUP, GROUP))

def reference(tokens, weight, momentum, grad, selection):
    basis = dct_matrix()
    moment = beta_decay * momentum + grad
    replicas = moment.shape[0]
    chosen_all = []
    new_moms = []
    for rep_index in range(replicas):
        blocks = to_groups(moment[rep_index])
        coeff = forward_dct(blocks, basis)
        coeff = coeff.reshape(coeff.shape[0], coeff.shape[1], GROUP * GROUP)
        chosen = jnp.take_along_axis(coeff, selection[rep_index], axis=-1)
        own = from_groups(inverse_dct(scatter_dense(selection[rep_index], chosen), basis))
        new_moms.append(moment[rep_index] - own)
        chosen_all.append(chosen)
    chosen_all = jnp.stack(chosen_all, 0)
    nrow, ncol = (selection.shape[1], selection.shape[2])
    joint_idx = jnp.moveaxis(selection, 0, 2).reshape(nrow, ncol, replicas * KEEP)
    joint_val = jnp.moveaxis(chosen_all, 0, 2).reshape(nrow, ncol, replicas * KEEP)
    update = from_groups(inverse_dct(scatter_dense(joint_idx, joint_val), basis))
    new_weight = (weight.astype(jnp.float32) - step_rate * update).astype(jnp.bfloat16)
    keys = jnp.dot(tokens, new_weight, preferred_element_type=jnp.float32).astype(jnp.bfloat16)
    return (keys, new_weight, jnp.stack(new_moms, 0))
```

```python
import functools

import jax
import jax.numpy as jnp
import numpy as np
from jax import lax
from jax.experimental import pallas as pl
from jax.experimental.pallas import tpu as pltpu
from jax.sharding import Mesh, PartitionSpec as P

GROUP = 64
KEEP = 64
REPS = 4
PAIR = 2 * GROUP

beta_decay = 0.999
step_rate = 0.05

HIGHEST = lax.Precision.HIGHEST
NT = (((1,), (1,)), ((), ()))


def dct_blocks(size):
    freq = np.arange(GROUP, dtype=np.float64)[:, None]
    place = np.arange(GROUP, dtype=np.float64)[None, :]
    scale = np.where(freq == 0, np.sqrt(1.0 / GROUP), np.sqrt(2.0 / GROUP))
    basis = scale * np.cos(np.pi * (2.0 * place + 1.0) * freq / (2.0 * GROUP))
    return np.kron(np.eye(size // GROUP), basis).astype(np.float32)


def halves(value):
    high = value.astype(jnp.bfloat16)
    return high, (value - high.astype(jnp.float32)).astype(jnp.bfloat16)


def targets(idx):
    lane = lax.broadcasted_iota(jnp.int32, idx.shape, 1)
    stacked = jnp.bitwise_and(jnp.right_shift(lane, 6), 3)
    return jnp.right_shift(idx, 6) + stacked * GROUP, jnp.bitwise_and(idx, GROUP - 1)


def is_row(target, rows):
    return lax.broadcasted_iota(jnp.int32, (rows, target.shape[1]), 0) == target


def coeff_kernel(momentum, grad, selection, basis, coeff, chosen, indices, held, sem):
    blocks = held.shape[1]
    first = ((lax.axis_index("y") * 4 + lax.axis_index("z")) * 2 + lax.axis_index("core")) * blocks
    copy = pltpu.make_async_copy(selection.at[:, pl.ds(first, blocks)], held, sem)
    copy.start()
    moment = beta_decay * momentum[0] + grad[0]
    inner = jnp.dot(basis[...], moment, precision=HIGHEST, preferred_element_type=jnp.float32)
    width = basis.shape[0]
    for c in range(0, moment.shape[1], width):
        coeff[:, c : c + width] = lax.dot_general(
            inner[:, c : c + width], basis[...], NT, precision=HIGHEST, preferred_element_type=jnp.float32
        )
    copy.wait()
    for r in range(REPS):
        indices[r] = jnp.concatenate([held[r, a] for a in range(blocks)], axis=1)
    row, col = targets(indices[lax.axis_index("x")])
    for p in range(coeff.shape[1] // PAIR):
        high, low = halves(coeff[:, p * PAIR : (p + 1) * PAIR])
        left = jnp.concatenate([high, low], axis=1)
        for b in range(2):
            k = 2 * p + b
            pick = jnp.where(is_row(col[k : k + 1] + b * GROUP, PAIR), 1.0, 0.0).astype(jnp.bfloat16)
            picked = jnp.dot(left, jnp.concatenate([pick, pick], axis=0), preferred_element_type=jnp.float32)
            mine = jnp.where(is_row(row[k : k + 1], picked.shape[0]), picked, 0.0)
            chosen[k : k + 1, :] = jnp.sum(mine, axis=0, keepdims=True)


def weight_kernel(weight, values, indices, basis, new_weight, dense):
    rows = weight.shape[0]
    for p in range(weight.shape[1] // PAIR):
        lefts, highs, lows = [], [], []
        for b in range(2):
            k = 2 * p + b
            for r in range(REPS):
                row, col = targets(indices[r, k : k + 1, :])
                lefts.append(jnp.where(is_row(row, rows), 1.0, 0.0).astype(jnp.bfloat16))
                here = is_row(col + b * GROUP, PAIR)
                high, low = halves(values[r, k : k + 1, :])
                highs.append(jnp.where(here, high.astype(jnp.float32), 0.0).astype(jnp.bfloat16))
                lows.append(jnp.where(here, low.astype(jnp.float32), 0.0).astype(jnp.bfloat16))
        right = jnp.concatenate([jnp.concatenate(highs, axis=1), jnp.concatenate(lows, axis=1)], axis=0)
        both = lax.dot_general(jnp.concatenate(lefts, axis=1), right, NT, preferred_element_type=jnp.float32)
        dense[:, p * PAIR : (p + 1) * PAIR] = both[:, :PAIR] + both[:, PAIR:]
    width = basis.shape[0]
    inner = jnp.dot(basis[...].T, dense[...], precision=HIGHEST, preferred_element_type=jnp.float32)
    for c in range(0, weight.shape[1], width):
        update = jnp.dot(inner[:, c : c + width], basis[...], precision=HIGHEST, preferred_element_type=jnp.float32)
        old = weight[:, c : c + width].astype(jnp.float32)
        new_weight[:, c : c + width] = (old - step_rate * update).astype(jnp.bfloat16)


def momentum_kernel(momentum, grad, coeff, indices, basis, new_momentum, dense):
    rows = coeff.shape[0]
    row, col = targets(indices[lax.axis_index("x")])
    for p in range(coeff.shape[1] // PAIR):
        lefts, rights = [], []
        for b in range(2):
            k = 2 * p + b
            lefts.append(jnp.where(is_row(row[k : k + 1], rows), 1.0, 0.0).astype(jnp.bfloat16))
            rights.append(jnp.where(is_row(col[k : k + 1] + b * GROUP, PAIR), 1.0, 0.0).astype(jnp.bfloat16))
        kept = lax.dot_general(
            jnp.concatenate(lefts, axis=1), jnp.concatenate(rights, axis=1), NT, preferred_element_type=jnp.float32
        )
        dense[:, p * PAIR : (p + 1) * PAIR] = jnp.where(kept > 0.5, coeff[:, p * PAIR : (p + 1) * PAIR], 0.0)
    width = basis.shape[0]
    inner = jnp.dot(basis[...].T, dense[...], precision=HIGHEST, preferred_element_type=jnp.float32)
    for c in range(0, coeff.shape[1], width):
        own = jnp.dot(inner[:, c : c + width], basis[...], precision=HIGHEST, preferred_element_type=jnp.float32)
        moment = beta_decay * momentum[0, :, c : c + width] + grad[0, :, c : c + width]
        new_momentum[0, :, c : c + width] = moment - own


VM = pl.BlockSpec(memory_space=pltpu.VMEM)
HBM = pl.BlockSpec(memory_space=pl.ANY)
PARAMS = pltpu.CompilerParams(vmem_limit_bytes=48 * 2**20)


def on_device(tokens, weight, momentum, grad, selection):
    rows, cols = weight.shape
    blocks = rows // GROUP
    basis = jnp.asarray(dct_blocks(rows))
    coeff, chosen, indices = pl.pallas_call(
        coeff_kernel,
        out_shape=(
            jax.ShapeDtypeStruct((rows, cols), jnp.float32),
            jax.ShapeDtypeStruct((cols // GROUP, blocks * KEEP), jnp.float32),
            jax.ShapeDtypeStruct((REPS, cols // GROUP, blocks * KEEP), jnp.int32),
        ),
        in_specs=[VM, VM, HBM, VM],
        out_specs=(VM, VM, VM),
        scratch_shapes=[pltpu.VMEM((REPS, blocks, cols // GROUP, KEEP), jnp.int32), pltpu.SemaphoreType.DMA],
        compiler_params=PARAMS,
    )(momentum, grad, selection, basis)
    everyone = lax.all_gather(chosen, "x", axis=0)
    new_weight = pl.pallas_call(
        weight_kernel,
        out_shape=jax.ShapeDtypeStruct((rows, cols), jnp.bfloat16),
        in_specs=[VM] * 4,
        out_specs=VM,
        scratch_shapes=[pltpu.VMEM((rows, cols), jnp.float32)],
        compiler_params=PARAMS,
    )(weight, everyone, indices, basis)
    new_momentum = pl.pallas_call(
        momentum_kernel,
        out_shape=jax.ShapeDtypeStruct(momentum.shape, jnp.float32),
        in_specs=[VM] * 5,
        out_specs=VM,
        scratch_shapes=[pltpu.VMEM((rows, cols), jnp.float32)],
        compiler_params=PARAMS,
    )(momentum, grad, coeff, indices, basis)
    keys = jnp.dot(
        tokens,
        lax.all_gather(new_weight, ("y", "z", "core"), axis=0, tiled=True),
        preferred_element_type=jnp.float32,
    )
    return (keys.astype(jnp.bfloat16), new_weight, new_momentum)


def solution(mesh):
    chips = Mesh(mesh.devices.reshape(4, 4, 4, 2), ("x", "y", "z", "core"))
    plane = ("y", "z", "core")
    return jax.shard_map(
        on_device,
        mesh=chips,
        in_specs=(
            P(("x",) + plane, None),
            P(plane, None),
            P("x", plane, None),
            P("x", plane, None),
            P(),
        ),
        out_specs=(P(("x",) + plane, None), P(plane, None), P("x", plane, None)),
        check_vma=False,
    )
```

```python
import jax
import jax.numpy as jnp
import numpy as np
from jax import lax
from jax.experimental import pallas as pl
from jax.experimental.pallas import tpu as pltpu
from jax.sharding import Mesh, PartitionSpec as P

GROUP = 64
KEEP = 64
REPS = 4
SIDE = 4
PAIR = 2 * GROUP
PLANE = ("y", "z", "core")

beta_decay = 0.999
step_rate = 0.05

HIGHEST = lax.Precision.HIGHEST
NT = (((1,), (1,)), ((), ()))
TN = (((0,), (0,)), ((), ()))
VM = pl.BlockSpec(memory_space=pltpu.VMEM)
HBM = pl.BlockSpec(memory_space=pltpu.HBM)
PARAMS = pltpu.CompilerParams(vmem_limit_bytes=32 * 2**20)
ALONE = pltpu.CompilerParams(vmem_limit_bytes=60 * 2**20)
FLOPS, BYTES = 1000, 1000


def dct_blocks(size):
    freq = np.arange(GROUP, dtype=np.float64)[:, None]
    place = np.arange(GROUP, dtype=np.float64)[None, :]
    scale = np.where(freq == 0, np.sqrt(1.0 / GROUP), np.sqrt(2.0 / GROUP))
    basis = scale * np.cos(np.pi * (2.0 * place + 1.0) * freq / (2.0 * GROUP))
    return np.kron(np.eye(size // GROUP), basis).astype(np.float32)


def halves(value):
    high = value.astype(jnp.bfloat16)
    return high, (value - high.astype(jnp.float32)).astype(jnp.bfloat16)


def dot3(left, right, dims):
    total = None
    for a, b in ((0, 0), (0, 1), (1, 0)):
        part = lax.dot_general(left[a], right[b], dims, preferred_element_type=jnp.float32)
        total = part if total is None else total + part
    return total


def plain(contract):
    return (contract, ((), ()))


def is_row(target, rows):
    return lax.broadcasted_iota(jnp.int32, (rows, target.shape[1]), 0) == target


def one_hot(target, rows):
    return jnp.where(is_row(target, rows), 1.0, 0.0).astype(jnp.bfloat16)


def coeff_kernel(momentum, grad, selection, basis, chosen, where, mom, gra, sel, sems):
    blocks = mom.shape[0] // GROUP
    copies = [
        pltpu.make_async_copy(selection, sel, sems.at[0]),
        pltpu.make_async_copy(momentum.at[0], mom, sems.at[1]),
        pltpu.make_async_copy(grad.at[0], gra, sems.at[2]),
    ]
    for copy in copies:
        copy.start()
    base = basis[...]
    base = halves(base)
    first = ((lax.axis_index("y") * SIDE + lax.axis_index("z")) * 2 + lax.axis_index("core")) * blocks
    lanes = sel.shape[3]
    cols = sel.shape[1] * KEEP
    sub = lax.broadcasted_iota(jnp.int32, (16, 2 * lanes), 0)
    lane = lax.broadcasted_iota(jnp.int32, (16, 2 * lanes), 1)
    mine = jnp.where(sub < 8, first + sub, lanes + first + sub - 8)
    pick = jnp.where((lane == mine) & (jnp.bitwise_and(sub, 7) < blocks), 1.0, 0.0).astype(jnp.bfloat16)
    copies[0].wait()
    shift = jnp.bitwise_and(lax.broadcasted_iota(jnp.int32, (8, cols), 1), GROUP)
    for r in range(REPS):
        flat = sel[r].reshape(cols, lanes)
        row = jnp.right_shift(flat, 6).astype(jnp.float32).astype(jnp.bfloat16)
        col = jnp.bitwise_and(flat, GROUP - 1).astype(jnp.float32).astype(jnp.bfloat16)
        both = lax.dot_general(pick, jnp.concatenate([row, col], axis=1), NT, preferred_element_type=jnp.float32)
        both = both.astype(jnp.int32)
        where[0, r] = both[:8]
        where[1, r] = both[8:] + shift
    copies[1].wait()
    copies[2].wait()
    moment = halves(beta_decay * mom[...] + gra[...])
    inner = halves(dot3(base, moment, plain(((1,), (0,)))))
    own = lax.axis_index("x")
    width = base[0].shape[0]
    for c in range(0, mom.shape[1], width):
        coeff = dot3([part[:, c : c + width] for part in inner], base, NT)
        high, low = halves(coeff)
        for p in range(c, c + width, PAIR):
            span = slice(p - c, p - c + PAIR)
            for a in range(blocks):
                rows = slice(a * GROUP, (a + 1) * GROUP)
                left = jnp.concatenate([high[rows, span], low[rows, span]], axis=1)
                right = one_hot(where[1, own, a : a + 1, p : p + PAIR], PAIR)
                found = jnp.dot(left, jnp.concatenate([right, right], axis=0), preferred_element_type=jnp.float32)
                kept = jnp.where(is_row(where[0, own, a : a + 1, p : p + PAIR], GROUP), found, 0.0)
                chosen[a : a + 1, p : p + PAIR] = jnp.sum(kept, axis=0, keepdims=True)


def weight_kernel(weight, chosen0, chosen1, chosen2, chosen3, where, basis, new_weight, dense):
    rows, cols = weight.shape
    here = lax.axis_index("x")
    base = halves(basis[...])
    values = []
    for k, chosen in enumerate((chosen0, chosen1, chosen2, chosen3)):
        high, low = halves(chosen[...])
        values.append((lax.rem(here - k + REPS, REPS), high.astype(jnp.float32), low.astype(jnp.float32)))
    for p in range(0, cols, PAIR):
        for a in range(rows // GROUP):
            lefts, highs, lows = [], [], []
            for r, high, low in values:
                lefts.append(one_hot(where[0, r, a : a + 1, p : p + PAIR], GROUP))
                hit = is_row(where[1, r, a : a + 1, p : p + PAIR], PAIR)
                highs.append(jnp.where(hit, high[a : a + 1, p : p + PAIR], 0.0).astype(jnp.bfloat16))
                lows.append(jnp.where(hit, low[a : a + 1, p : p + PAIR], 0.0).astype(jnp.bfloat16))
            right = jnp.concatenate([jnp.concatenate(highs, axis=1), jnp.concatenate(lows, axis=1)], axis=0)
            both = lax.dot_general(jnp.concatenate(lefts, axis=1), right, NT, preferred_element_type=jnp.float32)
            dense[a * GROUP : (a + 1) * GROUP, p : p + PAIR] = both[:, :PAIR] + both[:, PAIR:]
    inner = halves(dot3(base, halves(dense[...]), TN))
    width = rows
    for c in range(0, cols, width):
        update = dot3([part[:, c : c + width] for part in inner], base, plain(((1,), (0,))))
        old = weight[:, c : c + width].astype(jnp.float32)
        new_weight[:, c : c + width] = (old - step_rate * update).astype(jnp.bfloat16)


def momentum_kernel(momentum, grad, where, basis, new_momentum, dense):
    rows, cols = dense.shape
    own = lax.axis_index("x")
    base = basis[...]
    moment = beta_decay * momentum[0] + grad[0]
    inner = jnp.dot(base, moment, precision=HIGHEST, preferred_element_type=jnp.float32)
    width = rows
    for c in range(0, cols, width):
        coeff = lax.dot_general(inner[:, c : c + width], base, NT, precision=HIGHEST, preferred_element_type=jnp.float32)
        for p in range(c, c + width, PAIR):
            for a in range(rows // GROUP):
                left = one_hot(where[0, own, a : a + 1, p : p + PAIR], GROUP)
                right = one_hot(where[1, own, a : a + 1, p : p + PAIR], PAIR)
                kept = lax.dot_general(left, right, NT, preferred_element_type=jnp.float32)
                span = slice(a * GROUP, (a + 1) * GROUP)
                dense[span, p : p + PAIR] = jnp.where(kept > 0.5, coeff[span, p - c : p - c + PAIR], 0.0)
    inner = lax.dot_general(base, dense[...], TN, precision=HIGHEST, preferred_element_type=jnp.float32)
    for c in range(0, cols, width):
        own_part = jnp.dot(inner[:, c : c + width], base, precision=HIGHEST, preferred_element_type=jnp.float32)
        moment = beta_decay * momentum[0, :, c : c + width] + grad[0, :, c : c + width]
        new_momentum[0, :, c : c + width] = moment - own_part


def ring(axis, step):
    pairs = []
    for y in range(SIDE):
        for z in range(SIDE):
            for c in range(2):
                if (c == 0) == (axis == "u"):
                    to = ((y + step) % SIDE, z)
                else:
                    to = (y, (z + step) % SIDE)
                pairs.append(((y * SIDE + z) * 2 + c, (to[0] * SIDE + to[1]) * 2 + c))
    return pairs


def send(value, axis, step):
    return lax.ppermute(value, PLANE, ring(axis, step))


def sibling(value):
    return lax.ppermute(value, "core", [(0, 1), (1, 0)])


def shard_at(u, v, other=False):
    y, z, c = lax.axis_index("y"), lax.axis_index("z"), lax.axis_index("core")
    if other:
        c = 1 - c
    along = lambda at, step: lax.rem(at + step + SIDE, SIDE)
    even = along(y, u) * SIDE + along(z, v)
    odd = along(y, v) * SIDE + along(z, u)
    return 2 * jnp.where(c == 0, even, odd) + c


def multiply(jobs, shards, pieces, dtypes, after=None, chunks=((0, 1024),)):
    cols = pieces[0].shape[1]
    depth, tile = 256, 256
    count = len(shards)
    rows = jobs[0][0].shape[0]
    after = jnp.zeros((8, 128), jnp.float32) if after is None else after
    adds = [x for _, some in jobs for x in some]
    n_jobs, n_pieces, n_adds = len(jobs), len(pieces), len(adds)
    aliases, at = {}, 2 + n_jobs + n_pieces
    for n, (_, some) in enumerate(jobs):
        if some and some[0].dtype == dtypes[n]:
            aliases[at] = n
        at += len(some)

    def kernel(ids, _, *refs):
        toks, refs = refs[:n_jobs], refs[n_jobs:]
        ws, refs = refs[:n_pieces], refs[n_pieces:]
        adds, refs = refs[:n_adds], refs[n_adds:]
        outs, (ran, left, right, sems, piece_sems) = refs[:n_jobs], refs[n_jobs:]
        ran[...] = jnp.zeros_like(ran)
        loads, at = [], 0
        for k, w in enumerate(ws):
            deep = w.shape[0]
            loads.append(pltpu.make_async_copy(w, right.at[pl.ds(at, deep)], piece_sems.at[k]))
            loads[-1].start()
            at += deep
        plan = [(n, at, size) for n in range(n_jobs) for at, size in chunks]
        copies = {}

        def issue(q):
            n, at, size = plan[q]
            for k in range(count):
                copies[q, k] = pltpu.make_async_copy(
                    toks[n].at[pl.ds(at, size), pl.ds(pl.multiple_of(ids[k] * depth, depth), depth)],
                    left.at[n, pl.ds(at, size), pl.ds(k * depth, depth)],
                    sems.at[q, k],
                )
                copies[q, k].start()

        issue(0)
        for load in loads:
            load.wait()
        for q, (n, at, size) in enumerate(plan):
            for k in range(count):
                copies[q, k].wait()
            if q + 1 < len(plan):
                issue(q + 1)
            first = sum(len(some) for _, some in jobs[:n])
            mine = adds[first : first + len(jobs[n][1])]
            for i in range(at, at + size, tile):
                span = slice(i, i + tile)
                result = jnp.dot(left[n, span, :], right[...], preferred_element_type=jnp.float32)
                for add in mine:
                    result = result + add[span, :].astype(jnp.float32)
                outs[n][span, :] = result.astype(outs[n].dtype)

    def result(dtype):
        shape = (rows, cols)
        return pltpu.VMEM(shape, dtype) if dtype == jnp.float32 else jax.ShapeDtypeStruct(shape, dtype)

    return pl.pallas_call(
        kernel,
        in_specs=[pl.BlockSpec(memory_space=pltpu.SMEM)] + [HBM] * (1 + n_jobs + n_pieces) + [VM] * n_adds,
        out_specs=[VM] * (n_jobs + 1),
        out_shape=[result(dtype) for dtype in dtypes] + [jax.ShapeDtypeStruct((8, 128), jnp.float32)],
        scratch_shapes=[
            pltpu.VMEM((n_jobs, rows, count * depth), jnp.bfloat16),
            pltpu.VMEM((count * depth, cols), jnp.bfloat16),
            pltpu.SemaphoreType.DMA((n_jobs * len(chunks), count)),
            pltpu.SemaphoreType.DMA((n_pieces,)),
        ],
        compiler_params=pltpu.CompilerParams(vmem_limit_bytes=24 * 2**20),
        cost_estimate=pl.CostEstimate(flops=FLOPS, bytes_accessed=BYTES, transcendentals=0),
        input_output_aliases=aliases,
    )(jnp.stack(shards).astype(jnp.int32), after, *[in_hbm(t) for t, _ in jobs], *[in_hbm(p) for p in pieces], *adds)


def in_hbm(value):
    return pltpu.with_memory_space_constraint(value, pltpu.HBM)


def on_device(tokens, weight, momentum, grad, selection):
    rows, cols = weight.shape
    blocks = rows // GROUP
    basis = jnp.asarray(dct_blocks(rows))
    lanes = selection.transpose(0, 2, 3, 1)
    chosen, where = pl.pallas_call(
        coeff_kernel,
        out_shape=(
            jax.ShapeDtypeStruct((blocks, cols), jnp.float32),
            jax.ShapeDtypeStruct((2, REPS, 8, cols), jnp.int32),
        ),
        in_specs=[HBM, HBM, HBM, VM],
        out_specs=(VM, VM),
        scratch_shapes=[
            pltpu.VMEM((rows, cols), jnp.float32),
            pltpu.VMEM((rows, cols), jnp.float32),
            pltpu.VMEM(lanes.shape, jnp.int32),
            pltpu.SemaphoreType.DMA((3,)),
        ],
        compiler_params=PARAMS,
    )(in_hbm(momentum), in_hbm(grad), in_hbm(lanes), basis)
    along_x = lambda step: lax.ppermute(chosen, "x", [(i, (i + step) % REPS) for i in range(REPS)])
    others = [along_x(k) for k in range(1, REPS)]
    tokens_too = sibling(tokens)
    shard = pl.pallas_call(
        weight_kernel,
        out_shape=jax.ShapeDtypeStruct((rows, cols), jnp.bfloat16),
        in_specs=[VM] * 7,
        out_specs=VM,
        scratch_shapes=[pltpu.VMEM((rows, cols), jnp.float32)],
        compiler_params=PARAMS,
    )(weight, chosen, *others, where, basis)

    am, ap = send(shard, "u", 1), send(shard, "u", -1)
    new_momentum = pl.pallas_call(
        momentum_kernel,
        out_shape=jax.ShapeDtypeStruct(momentum.shape, jnp.float32),
        in_specs=[VM] * 4,
        out_specs=VM,
        scratch_shapes=[pltpu.VMEM((rows, cols), jnp.float32)],
        compiler_params=PARAMS,
    )(momentum, grad, where, basis)
    am, ap, new_momentum = lax.optimization_barrier((am, ap, new_momentum))
    top, bottom = send(am[: rows // 2], "u", 1), send(ap[rows // 2 :], "u", -1)
    s1 = jnp.concatenate([shard, am], axis=0)
    s2 = jnp.concatenate([ap, top, bottom], axis=0)
    r1p, r2m = send(s1, "v", 1), send(s2, "v", -1)
    r2p, r1m = send(s2, "v", 1), send(s1, "v", -1)
    f32, bf16 = jnp.float32, jnp.bfloat16
    mine, theirs, ran = multiply(
        [(tokens, ()), (tokens_too, ())],
        [shard_at(0, 0), shard_at(-1, 0), shard_at(1, 0), shard_at(2, 0)],
        [s1, s2],
        [f32, f32],
    )
    r1p, r2m, ran = lax.optimization_barrier((r1p, r2m, ran))
    f1, f2 = send(r1p, "v", 1), send(r2m, "v", -1)
    mine, theirs, ran = multiply(
        [(tokens, (mine,)), (tokens_too, (theirs,))],
        [shard_at(0, -1), shard_at(-1, -1), shard_at(1, 1), shard_at(2, 1)],
        [r1p, r2m],
        [f32, f32],
        after=ran,
    )
    mine, theirs, ran = multiply(
        [(tokens, (mine,)), (tokens_too, (theirs,))],
        [shard_at(1, -1), shard_at(2, -1), shard_at(0, 1), shard_at(-1, 1)],
        [r2p, r1m],
        [f32, bf16],
        after=ran,
    )
    theirs = sibling(theirs)
    f1, f2, ran = lax.optimization_barrier((f1, f2, ran))
    g1, g2 = sibling(f1), sibling(f2)
    far = [(0, 2), (-1, 2), (1, 2), (2, 2)]
    split = ((0, 256), (256, 768))
    mine, ran = multiply([(tokens, (mine,))], [shard_at(*at) for at in far], [f1, f2], [f32], ran, split)
    keys, _ = multiply(
        [(tokens, (mine, theirs))], [shard_at(*at, other=True) for at in far], [g1, g2], [bf16], ran, split
    )
    return keys, shard, new_momentum


def solution(mesh):
    chips = Mesh(mesh.devices.reshape(REPS, SIDE, SIDE, 2), ("x",) + PLANE)
    return jax.shard_map(
        on_device,
        mesh=chips,
        in_specs=(
            P(("x",) + PLANE, None),
            P(PLANE, None),
            P("x", PLANE, None),
            P("x", PLANE, None),
            P(),
        ),
        out_specs=(P(("x",) + PLANE, None), P(PLANE, None), P("x", PLANE, None)),
        check_vma=False,
    )
```

```python
import jax
import jax.numpy as jnp
import numpy as np
from jax import lax
from jax.experimental import pallas as pl
from jax.experimental.pallas import tpu as pltpu
from jax.sharding import Mesh, PartitionSpec as P

GROUP = 64
KEEP = 64
REPS = 4
SIDE = 4
PAIR = 2 * GROUP
PLANE = ("y", "z", "core")

beta_decay = 0.999
step_rate = 0.05

HIGHEST = lax.Precision.HIGHEST
NT = (((1,), (1,)), ((), ()))
TN = (((0,), (0,)), ((), ()))
VM = pl.BlockSpec(memory_space=pltpu.VMEM)
ANY = pl.BlockSpec(memory_space=pl.ANY)
PARAMS = pltpu.CompilerParams(vmem_limit_bytes=32 * 2**20)
ALONE = pltpu.CompilerParams(vmem_limit_bytes=60 * 2**20)
SMALL = pl.CostEstimate(flops=1000, bytes_accessed=1000, transcendentals=0)


def dct_blocks(size):
    freq = np.arange(GROUP, dtype=np.float64)[:, None]
    place = np.arange(GROUP, dtype=np.float64)[None, :]
    scale = np.where(freq == 0, np.sqrt(1.0 / GROUP), np.sqrt(2.0 / GROUP))
    basis = scale * np.cos(np.pi * (2.0 * place + 1.0) * freq / (2.0 * GROUP))
    return np.kron(np.eye(size // GROUP), basis).astype(np.float32)


def halves(value):
    high = value.astype(jnp.bfloat16)
    return high, (value - high.astype(jnp.float32)).astype(jnp.bfloat16)


def dot3(left, right, dims):
    total = None
    for a, b in ((0, 0), (0, 1), (1, 0)):
        part = lax.dot_general(left[a], right[b], dims, preferred_element_type=jnp.float32)
        total = part if total is None else total + part
    return total


def plain(contract):
    return (contract, ((), ()))


def is_row(target, rows):
    return lax.broadcasted_iota(jnp.int32, (rows, target.shape[1]), 0) == target


def one_hot(target, rows):
    return jnp.where(is_row(target, rows), 1.0, 0.0).astype(jnp.bfloat16)


def coeff_kernel(momentum, grad, selection, basis, chosen, where, mom, gra, sel, dct, sems):
    blocks = mom.shape[0] // GROUP
    copies = [
        pltpu.make_async_copy(selection, sel, sems.at[0]),
        pltpu.make_async_copy(momentum.at[0], mom, sems.at[1]),
        pltpu.make_async_copy(grad.at[0], gra, sems.at[2]),
        pltpu.make_async_copy(basis, dct, sems.at[3]),
    ]
    for copy in copies:
        copy.start()
    first = ((lax.axis_index("y") * SIDE + lax.axis_index("z")) * 2 + lax.axis_index("core")) * blocks
    lanes = sel.shape[3]
    cols = sel.shape[1] * KEEP
    sub = lax.broadcasted_iota(jnp.int32, (16, 2 * lanes), 0)
    lane = lax.broadcasted_iota(jnp.int32, (16, 2 * lanes), 1)
    mine = jnp.where(sub < 8, first + sub, lanes + first + sub - 8)
    pick = jnp.where((lane == mine) & (jnp.bitwise_and(sub, 7) < blocks), 1.0, 0.0).astype(jnp.bfloat16)
    copies[0].wait()
    shift = jnp.bitwise_and(lax.broadcasted_iota(jnp.int32, (8, cols), 1), GROUP)
    for r in range(REPS):
        flat = sel[r].reshape(cols, lanes)
        row = jnp.right_shift(flat, 6).astype(jnp.float32).astype(jnp.bfloat16)
        col = jnp.bitwise_and(flat, GROUP - 1).astype(jnp.float32).astype(jnp.bfloat16)
        both = lax.dot_general(pick, jnp.concatenate([row, col], axis=1), NT, preferred_element_type=jnp.float32)
        both = both.astype(jnp.int32)
        where[0, r] = both[:8]
        where[1, r] = both[8:] + shift
    for copy in copies[1:]:
        copy.wait()
    base = halves(dct[...])
    moment = halves(beta_decay * mom[...] + gra[...])
    inner = halves(dot3(base, moment, plain(((1,), (0,)))))
    own = lax.axis_index("x")
    width = base[0].shape[0]
    for c in range(0, mom.shape[1], width):
        coeff = dot3([part[:, c : c + width] for part in inner], base, NT)
        high, low = halves(coeff)
        for p in range(c, c + width, PAIR):
            span = slice(p - c, p - c + PAIR)
            for a in range(blocks):
                rows = slice(a * GROUP, (a + 1) * GROUP)
                left = jnp.concatenate([high[rows, span], low[rows, span]], axis=1)
                right = one_hot(where[1, own, a : a + 1, p : p + PAIR], PAIR)
                found = jnp.dot(left, jnp.concatenate([right, right], axis=0), preferred_element_type=jnp.float32)
                kept = jnp.where(is_row(where[0, own, a : a + 1, p : p + PAIR], GROUP), found, 0.0)
                chosen[a : a + 1, p : p + PAIR] = jnp.sum(kept, axis=0, keepdims=True)


def weight_kernel(weight, chosen0, chosen1, chosen2, chosen3, where, basis, new_weight, dense):
    rows, cols = weight.shape
    here = lax.axis_index("x")
    base = halves(basis[...])
    values = []
    for k, chosen in enumerate((chosen0, chosen1, chosen2, chosen3)):
        high, low = halves(chosen[...])
        values.append((lax.rem(here - k + REPS, REPS), high.astype(jnp.float32), low.astype(jnp.float32)))
    for p in range(0, cols, PAIR):
        for a in range(rows // GROUP):
            lefts, highs, lows = [], [], []
            for r, high, low in values:
                lefts.append(one_hot(where[0, r, a : a + 1, p : p + PAIR], GROUP))
                hit = is_row(where[1, r, a : a + 1, p : p + PAIR], PAIR)
                highs.append(jnp.where(hit, high[a : a + 1, p : p + PAIR], 0.0).astype(jnp.bfloat16))
                lows.append(jnp.where(hit, low[a : a + 1, p : p + PAIR], 0.0).astype(jnp.bfloat16))
            right = jnp.concatenate([jnp.concatenate(highs, axis=1), jnp.concatenate(lows, axis=1)], axis=0)
            both = lax.dot_general(jnp.concatenate(lefts, axis=1), right, NT, preferred_element_type=jnp.float32)
            dense[a * GROUP : (a + 1) * GROUP, p : p + PAIR] = both[:, :PAIR] + both[:, PAIR:]
    inner = halves(dot3(base, halves(dense[...]), TN))
    width = rows
    for c in range(0, cols, width):
        update = dot3([part[:, c : c + width] for part in inner], base, plain(((1,), (0,))))
        old = weight[:, c : c + width].astype(jnp.float32)
        new_weight[:, c : c + width] = (old - step_rate * update).astype(jnp.bfloat16)


def momentum_kernel(momentum, grad, where, basis, new_momentum, dense):
    rows, cols = dense.shape
    own = lax.axis_index("x")
    base = basis[...]
    moment = beta_decay * momentum[0] + grad[0]
    inner = jnp.dot(base, moment, precision=HIGHEST, preferred_element_type=jnp.float32)
    width = rows
    for c in range(0, cols, width):
        coeff = lax.dot_general(inner[:, c : c + width], base, NT, precision=HIGHEST, preferred_element_type=jnp.float32)
        for p in range(c, c + width, PAIR):
            for a in range(rows // GROUP):
                left = one_hot(where[0, own, a : a + 1, p : p + PAIR], GROUP)
                right = one_hot(where[1, own, a : a + 1, p : p + PAIR], PAIR)
                kept = lax.dot_general(left, right, NT, preferred_element_type=jnp.float32)
                span = slice(a * GROUP, (a + 1) * GROUP)
                dense[span, p : p + PAIR] = jnp.where(kept > 0.5, coeff[span, p - c : p - c + PAIR], 0.0)
    inner = lax.dot_general(base, dense[...], TN, precision=HIGHEST, preferred_element_type=jnp.float32)
    for c in range(0, cols, width):
        own_part = jnp.dot(inner[:, c : c + width], base, precision=HIGHEST, preferred_element_type=jnp.float32)
        moment = beta_decay * momentum[0, :, c : c + width] + grad[0, :, c : c + width]
        new_momentum[0, :, c : c + width] = moment - own_part


def ring(axis, step):
    pairs = []
    for y in range(SIDE):
        for z in range(SIDE):
            for c in range(2):
                if (c == 0) == (axis == "u"):
                    to = ((y + step) % SIDE, z)
                else:
                    to = (y, (z + step) % SIDE)
                pairs.append(((y * SIDE + z) * 2 + c, (to[0] * SIDE + to[1]) * 2 + c))
    return pairs


def send(value, axis, step):
    return lax.ppermute(value, PLANE, ring(axis, step))


def sibling(value):
    return lax.ppermute(value, "core", [(0, 1), (1, 0)])


def shard_places():
    y, z, c = lax.axis_index("y"), lax.axis_index("z"), lax.axis_index("core")
    k = np.arange(2 * SIDE * SIDE)
    u, v = jnp.asarray(k // SIDE % SIDE, jnp.int32), jnp.asarray(k % SIDE, jnp.int32)
    core = jnp.where(jnp.asarray(k < SIDE * SIDE), c, 1 - c)
    even = jnp.bitwise_and(y + u, 3) * SIDE + jnp.bitwise_and(z + v, 3)
    odd = jnp.bitwise_and(y + v, 3) * SIDE + jnp.bitwise_and(z + u, 3)
    return 2 * jnp.where(core == 0, even, odd) + core


def at(*offsets, other=False):
    return [(u % SIDE) * SIDE + v % SIDE + (SIDE * SIDE if other else 0) for u, v in offsets]


def multiply(places, jobs, shards, pieces, dtypes, after=None, chunks=((0, 1024),)):
    cols = pieces[0].shape[1]
    depth, tile = 256, 256
    count = len(shards)
    rows = jobs[0][0].shape[0]
    after = jnp.zeros((8, 128), jnp.float32) if after is None else after
    adds = [x for _, some in jobs for x in some]
    n_jobs, n_pieces, n_adds = len(jobs), len(pieces), len(adds)
    aliases, at = {}, 2 + n_jobs + n_pieces
    for n, (_, some) in enumerate(jobs):
        if some and some[0].dtype == dtypes[n]:
            aliases[at] = n
        at += len(some)

    def kernel(ids, _, *refs):
        toks, refs = refs[:n_jobs], refs[n_jobs:]
        ws, refs = refs[:n_pieces], refs[n_pieces:]
        adds, refs = refs[:n_adds], refs[n_adds:]
        outs, (ran, left, right, sems, piece_sems) = refs[:n_jobs], refs[n_jobs:]
        ran[...] = jnp.zeros_like(ran)
        loads, at = [], 0
        for k, w in enumerate(ws):
            deep = w.shape[0]
            loads.append(pltpu.make_async_copy(w, right.at[pl.ds(at, deep)], piece_sems.at[k]))
            loads[-1].start()
            at += deep
        plan = [(n, at, size) for n in range(n_jobs) for at, size in chunks]
        copies = {}

        def issue(q):
            n, at, size = plan[q]
            for k in range(count):
                copies[q, k] = pltpu.make_async_copy(
                    toks[n].at[pl.ds(at, size), pl.ds(pl.multiple_of(ids[shards[k]] * depth, depth), depth)],
                    left.at[n, pl.ds(at, size), pl.ds(k * depth, depth)],
                    sems.at[q, k],
                )
                copies[q, k].start()

        issue(0)
        for load in loads:
            load.wait()
        for q, (n, at, size) in enumerate(plan):
            for k in range(count):
                copies[q, k].wait()
            if q + 1 < len(plan):
                issue(q + 1)
            first = sum(len(some) for _, some in jobs[:n])
            mine = adds[first : first + len(jobs[n][1])]
            for i in range(at, at + size, tile):
                span = slice(i, i + tile)
                result = jnp.dot(left[n, span, :], right[...], preferred_element_type=jnp.float32)
                for add in mine:
                    result = result + add[span, :].astype(jnp.float32)
                outs[n][span, :] = result.astype(outs[n].dtype)

    def result(dtype):
        shape = (rows, cols)
        return pltpu.VMEM(shape, dtype) if dtype == jnp.float32 else jax.ShapeDtypeStruct(shape, dtype)

    return pl.pallas_call(
        kernel,
        in_specs=[pl.BlockSpec(memory_space=pltpu.SMEM)] + [ANY] * (1 + n_jobs + n_pieces) + [VM] * n_adds,
        out_specs=[VM] * (n_jobs + 1),
        out_shape=[result(dtype) for dtype in dtypes] + [jax.ShapeDtypeStruct((8, 128), jnp.float32)],
        scratch_shapes=[
            pltpu.VMEM((n_jobs, rows, count * depth), jnp.bfloat16),
            pltpu.VMEM((count * depth, cols), jnp.bfloat16),
            pltpu.SemaphoreType.DMA((n_jobs * len(chunks), count)),
            pltpu.SemaphoreType.DMA((n_pieces,)),
        ],
        compiler_params=pltpu.CompilerParams(vmem_limit_bytes=16 * 2**20),
        cost_estimate=SMALL,
        input_output_aliases=aliases,
    )(places, after, *[in_hbm(t) for t, _ in jobs], *pieces, *adds)


def in_hbm(value):
    return pltpu.with_memory_space_constraint(value, pltpu.HBM)


def on_device(tokens, weight, momentum, grad, selection):
    rows, cols = weight.shape
    blocks = rows // GROUP
    basis = jnp.asarray(dct_blocks(rows))
    lanes = selection.transpose(0, 2, 3, 1)
    chosen, where = pl.pallas_call(
        coeff_kernel,
        out_shape=(
            jax.ShapeDtypeStruct((blocks, cols), jnp.float32),
            jax.ShapeDtypeStruct((2, REPS, 8, cols), jnp.int32),
        ),
        in_specs=[ANY] * 4,
        out_specs=(VM, VM),
        scratch_shapes=[
            pltpu.VMEM((rows, cols), jnp.float32),
            pltpu.VMEM((rows, cols), jnp.float32),
            pltpu.VMEM(lanes.shape, jnp.int32),
            pltpu.VMEM(basis.shape, jnp.float32),
            pltpu.SemaphoreType.DMA((4,)),
        ],
        compiler_params=PARAMS,
        cost_estimate=SMALL,
    )(in_hbm(momentum), in_hbm(grad), in_hbm(lanes), in_hbm(basis))
    along_x = lambda step: lax.ppermute(chosen, "x", [(i, (i + step) % REPS) for i in range(REPS)])
    others = [along_x(k) for k in range(1, REPS)]
    tokens_too = sibling(tokens)
    shard = pl.pallas_call(
        weight_kernel,
        out_shape=jax.ShapeDtypeStruct((rows, cols), jnp.bfloat16),
        in_specs=[VM] * 7,
        out_specs=VM,
        scratch_shapes=[pltpu.VMEM((rows, cols), jnp.float32)],
        compiler_params=PARAMS,
        cost_estimate=SMALL,
    )(weight, chosen, *others, where, basis)

    places = shard_places()
    am, ap = send(shard, "u", 1), send(shard, "u", -1)
    new_momentum = pl.pallas_call(
        momentum_kernel,
        out_shape=jax.ShapeDtypeStruct(momentum.shape, jnp.float32),
        in_specs=[VM] * 4,
        out_specs=VM,
        scratch_shapes=[pltpu.VMEM((rows, cols), jnp.float32)],
        compiler_params=PARAMS,
        cost_estimate=SMALL,
    )(momentum, grad, where, basis)
    am, ap, new_momentum = lax.optimization_barrier((am, ap, new_momentum))
    top, bottom = send(am[: rows // 2], "u", 1), send(ap[rows // 2 :], "u", -1)
    s1 = jnp.concatenate([shard, am], axis=0)
    r1p, r1m = send(s1, "v", 1), send(s1, "v", -1)
    f32, bf16 = jnp.float32, jnp.bfloat16
    mine, theirs, ran = multiply(
        places, [(tokens, ()), (tokens_too, ())], at((0, 0), (-1, 0)), [s1], [f32, f32]
    )
    top, bottom, ran = lax.optimization_barrier((top, bottom, ran))
    s2 = jnp.concatenate([ap, top, bottom], axis=0)
    r2p, r2m = send(s2, "v", 1), send(s2, "v", -1)
    f1 = send(r1p, "v", 1)
    mine, theirs, ran = multiply(
        places,
        [(tokens, (mine,)), (tokens_too, (theirs,))],
        at((1, 0), (2, 0), (0, -1), (-1, -1), (0, 1), (-1, 1)),
        [s2, r1p, r1m],
        [f32, f32],
        ran,
    )
    r2m, ran = lax.optimization_barrier((r2m, ran))
    f2 = send(r2m, "v", -1)
    mine, theirs, ran = multiply(
        places,
        [(tokens, (mine,)), (tokens_too, (theirs,))],
        at((1, -1), (2, -1), (1, 1), (2, 1)),
        [r2p, r2m],
        [f32, bf16],
        ran,
    )
    theirs = sibling(theirs)
    f1, ran = lax.optimization_barrier((f1, ran))
    g1 = sibling(f1)
    g2 = sibling(f2)
    near, far = [(0, 2), (-1, 2)], [(1, 2), (2, 2)]
    mine, ran = multiply(
        places, [(tokens, (mine,))], at(*near) + at(*near, other=True), [f1, g1], [f32], ran
    )
    keys, _ = multiply(
        places, [(tokens, (mine, theirs))], at(*far) + at(*far, other=True), [f2, g2], [bf16], ran
    )
    return keys, shard, new_momentum


def solution(mesh):
    chips = Mesh(mesh.devices.reshape(REPS, SIDE, SIDE, 2), ("x",) + PLANE)
    return jax.shard_map(
        on_device,
        mesh=chips,
        in_specs=(
            P(("x",) + PLANE, None),
            P(PLANE, None),
            P("x", PLANE, None),
            P("x", PLANE, None),
            P(),
        ),
        out_specs=(P(("x",) + PLANE, None), P(PLANE, None), P("x", PLANE, None)),
        check_vma=False,
    )
```

```python
import functools

import jax
import jax.numpy as jnp
import numpy as np
from jax import lax
from jax.experimental import pallas as pl
from jax.experimental.pallas import tpu as pltpu
from jax.sharding import Mesh, PartitionSpec as P

GROUP = 64
KEEP = 64
REPS = 4
SIDE = 4
PAIR = 2 * GROUP
PLANE = ("y", "z", "core")

beta_decay = 0.999
step_rate = 0.05

HIGHEST = lax.Precision.HIGHEST
NT = (((1,), (1,)), ((), ()))
TN = (((0,), (0,)), ((), ()))
VM = pl.BlockSpec(memory_space=pltpu.VMEM)
ANY = pl.BlockSpec(memory_space=pl.ANY)
PARAMS = pltpu.CompilerParams(vmem_limit_bytes=32 * 2**20)
ALONE = pltpu.CompilerParams(vmem_limit_bytes=60 * 2**20)
SMALL = pl.CostEstimate(flops=1000, bytes_accessed=1000, transcendentals=0)


def dct_blocks(size):
    freq = np.arange(GROUP, dtype=np.float64)[:, None]
    place = np.arange(GROUP, dtype=np.float64)[None, :]
    scale = np.where(freq == 0, np.sqrt(1.0 / GROUP), np.sqrt(2.0 / GROUP))
    basis = scale * np.cos(np.pi * (2.0 * place + 1.0) * freq / (2.0 * GROUP))
    return np.kron(np.eye(size // GROUP), basis).astype(np.float32)


def halves(value):
    high = value.astype(jnp.bfloat16)
    return high, (value - high.astype(jnp.float32)).astype(jnp.bfloat16)


def dot3(left, right, dims):
    total = None
    for a, b in ((0, 0), (0, 1), (1, 0)):
        part = lax.dot_general(left[a], right[b], dims, preferred_element_type=jnp.float32)
        total = part if total is None else total + part
    return total


def plain(contract):
    return (contract, ((), ()))


def is_row(target, rows):
    return lax.broadcasted_iota(jnp.int32, (rows, target.shape[1]), 0) == target


def one_hot(target, rows):
    return jnp.where(is_row(target, rows), 1.0, 0.0).astype(jnp.bfloat16)


def picker(blocks, lanes):
    first = ((lax.axis_index("y") * SIDE + lax.axis_index("z")) * 2 + lax.axis_index("core")) * blocks
    sub = lax.broadcasted_iota(jnp.int32, (16, 2 * lanes), 0)
    lane = lax.broadcasted_iota(jnp.int32, (16, 2 * lanes), 1)
    mine = jnp.where(sub < 8, first + sub, lanes + first + sub - 8)
    return jnp.where((lane == mine) & (jnp.bitwise_and(sub, 7) < blocks), 1.0, 0.0).astype(jnp.bfloat16)


def place_of(flat, pick, where, r):
    cols, lanes = flat.shape[0] * flat.shape[1], flat.shape[2]
    flat = flat.reshape(cols, lanes)
    row = jnp.right_shift(flat, 6).astype(jnp.float32).astype(jnp.bfloat16)
    col = jnp.bitwise_and(flat, GROUP - 1).astype(jnp.float32).astype(jnp.bfloat16)
    both = lax.dot_general(pick, jnp.concatenate([row, col], axis=1), NT, preferred_element_type=jnp.float32)
    both = both.astype(jnp.int32)
    where[0, r] = both[:8]
    where[1, r] = both[8:] + jnp.bitwise_and(lax.broadcasted_iota(jnp.int32, (8, cols), 1), GROUP)


def coeff_kernel(momentum, grad, selection, basis, chosen, where, mom, gra, sel, dct, sems):
    blocks = mom.shape[0] // GROUP
    copies = [
        pltpu.make_async_copy(selection.at[lax.axis_index("x")], sel, sems.at[0]),
        pltpu.make_async_copy(momentum.at[0], mom, sems.at[1]),
        pltpu.make_async_copy(grad.at[0], gra, sems.at[2]),
        pltpu.make_async_copy(basis, dct, sems.at[3]),
    ]
    for copy in copies:
        copy.start()
    pick = picker(blocks, sel.shape[2])
    copies[0].wait()
    place_of(sel[...], pick, where, 0)
    for copy in copies[1:]:
        copy.wait()
    base = halves(dct[...])
    moment = halves(beta_decay * mom[...] + gra[...])
    inner = halves(dot3(base, moment, plain(((1,), (0,)))))
    width = base[0].shape[0]
    for c in range(0, mom.shape[1], width):
        coeff = dot3([part[:, c : c + width] for part in inner], base, NT)
        high, low = halves(coeff)
        for p in range(c, c + width, PAIR):
            span = slice(p - c, p - c + PAIR)
            for a in range(blocks):
                rows = slice(a * GROUP, (a + 1) * GROUP)
                left = jnp.concatenate([high[rows, span], low[rows, span]], axis=1)
                right = one_hot(where[1, 0, a : a + 1, p : p + PAIR], PAIR)
                found = jnp.dot(left, jnp.concatenate([right, right], axis=0), preferred_element_type=jnp.float32)
                kept = jnp.where(is_row(where[0, 0, a : a + 1, p : p + PAIR], GROUP), found, 0.0)
                chosen[a : a + 1, p : p + PAIR] = jnp.sum(kept, axis=0, keepdims=True)


def others_kernel(blocks, selection, where, sel, sems):
    copies = []
    for k in range(REPS - 1):
        r = lax.rem(lax.axis_index("x") + REPS - 1 - k, REPS)
        copies.append(pltpu.make_async_copy(selection.at[r], sel.at[k], sems.at[k]))
        copies[-1].start()
    pick = picker(blocks, sel.shape[3])
    for k in range(REPS - 1):
        copies[k].wait()
        place_of(sel[k], pick, where, k)


def weight_kernel(weight, chosen0, chosen1, chosen2, chosen3, where, others, basis, new_weight, dense):
    rows, cols = weight.shape
    base = halves(basis[...])
    values = []
    for k, chosen in enumerate((chosen0, chosen1, chosen2, chosen3)):
        high, low = halves(chosen[...])
        values.append((others if k else where, max(k - 1, 0), high.astype(jnp.float32), low.astype(jnp.float32)))
    for p in range(0, cols, PAIR):
        for a in range(rows // GROUP):
            lefts, highs, lows = [], [], []
            for places, r, high, low in values:
                lefts.append(one_hot(places[0, r, a : a + 1, p : p + PAIR], GROUP))
                hit = is_row(places[1, r, a : a + 1, p : p + PAIR], PAIR)
                highs.append(jnp.where(hit, high[a : a + 1, p : p + PAIR], 0.0).astype(jnp.bfloat16))
                lows.append(jnp.where(hit, low[a : a + 1, p : p + PAIR], 0.0).astype(jnp.bfloat16))
            right = jnp.concatenate([jnp.concatenate(highs, axis=1), jnp.concatenate(lows, axis=1)], axis=0)
            both = lax.dot_general(jnp.concatenate(lefts, axis=1), right, NT, preferred_element_type=jnp.float32)
            dense[a * GROUP : (a + 1) * GROUP, p : p + PAIR] = both[:, :PAIR] + both[:, PAIR:]
    inner = halves(dot3(base, halves(dense[...]), TN))
    width = rows
    for c in range(0, cols, width):
        update = dot3([part[:, c : c + width] for part in inner], base, plain(((1,), (0,))))
        old = weight[:, c : c + width].astype(jnp.float32)
        new_weight[:, c : c + width] = (old - step_rate * update).astype(jnp.bfloat16)


def momentum_kernel(momentum, grad, where, basis, new_momentum, dense):
    rows, cols = dense.shape
    base = basis[...]
    moment = beta_decay * momentum[0] + grad[0]
    inner = jnp.dot(base, moment, precision=HIGHEST, preferred_element_type=jnp.float32)
    width = rows
    for c in range(0, cols, width):
        coeff = lax.dot_general(inner[:, c : c + width], base, NT, precision=HIGHEST, preferred_element_type=jnp.float32)
        for p in range(c, c + width, PAIR):
            for a in range(rows // GROUP):
                left = one_hot(where[0, 0, a : a + 1, p : p + PAIR], GROUP)
                right = one_hot(where[1, 0, a : a + 1, p : p + PAIR], PAIR)
                kept = lax.dot_general(left, right, NT, preferred_element_type=jnp.float32)
                span = slice(a * GROUP, (a + 1) * GROUP)
                dense[span, p : p + PAIR] = jnp.where(kept > 0.5, coeff[span, p - c : p - c + PAIR], 0.0)
    inner = lax.dot_general(base, dense[...], TN, precision=HIGHEST, preferred_element_type=jnp.float32)
    for c in range(0, cols, width):
        own_part = jnp.dot(inner[:, c : c + width], base, precision=HIGHEST, preferred_element_type=jnp.float32)
        moment = beta_decay * momentum[0, :, c : c + width] + grad[0, :, c : c + width]
        new_momentum[0, :, c : c + width] = moment - own_part


def ring(axis, step):
    pairs = []
    for y in range(SIDE):
        for z in range(SIDE):
            for c in range(2):
                if (c == 0) == (axis == "u"):
                    to = ((y + step) % SIDE, z)
                else:
                    to = (y, (z + step) % SIDE)
                pairs.append(((y * SIDE + z) * 2 + c, (to[0] * SIDE + to[1]) * 2 + c))
    return pairs


def send(value, axis, step):
    return lax.ppermute(value, PLANE, ring(axis, step))


def sibling(value):
    return lax.ppermute(value, "core", [(0, 1), (1, 0)])


def shard_places():
    y, z, c = lax.axis_index("y"), lax.axis_index("z"), lax.axis_index("core")
    k = np.arange(2 * SIDE * SIDE)
    u, v = jnp.asarray(k // SIDE % SIDE, jnp.int32), jnp.asarray(k % SIDE, jnp.int32)
    core = jnp.where(jnp.asarray(k < SIDE * SIDE), c, 1 - c)
    even = jnp.bitwise_and(y + u, 3) * SIDE + jnp.bitwise_and(z + v, 3)
    odd = jnp.bitwise_and(y + v, 3) * SIDE + jnp.bitwise_and(z + u, 3)
    return 2 * jnp.where(core == 0, even, odd) + core


def at(*offsets, other=False):
    return [(u % SIDE) * SIDE + v % SIDE + (SIDE * SIDE if other else 0) for u, v in offsets]


def multiply(places, jobs, shards, pieces, after=None, ahead=(), last=False, flops=1000):
    depth, tile = 256, 256
    rows, cols, count = jobs[0][0].shape[0], pieces[0].shape[1], len(shards)
    whole = [tok.shape[1] > count * depth for tok, _, _ in jobs]
    sources = [tok for (tok, _, _), w in zip(jobs, whole) if w] + [tok for tok, _ in ahead]
    laid = [tok for (tok, _, _), w in zip(jobs, whole) if not w]
    adds = [x for _, some, _ in jobs for x in some]
    n_jobs, n_whole = len(jobs), sum(whole)
    wide = max([len(some) for _, some in ahead], default=1)
    after = jnp.zeros((8, 128), jnp.float32) if after is None else after
    aliases, at = {}, 2 + len(sources) + len(pieces) + len(laid)
    for n, (_, some, dtype) in enumerate(jobs):
        if some and some[0].dtype == dtype:
            aliases[at] = n
        at += len(some)

    def kernel(ids, _, *refs):
        refs = list(refs)
        take = lambda n: [refs.pop(0) for _ in range(n)]
        srcs, ws, lefts, adds = take(len(sources)), take(len(pieces)), take(len(laid)), take(len(aliased))
        outs, nexts, (ran, *scratch) = take(n_jobs), take(len(ahead)), refs
        sems, next_sems, *left = scratch
        joined, loads, at = [], [], 0
        if len(ws) > 1:
            joined, piece_sems = [left.pop()], left.pop()
            for k, w in enumerate(ws):
                loads.append(pltpu.make_async_copy(w, joined[0].at[pl.ds(at, w.shape[0])], piece_sems.at[k]))
                loads[-1].start()
                at += w.shape[0]
        held, stores = outs, []
        if last:
            held, out_sems = [left.pop(0)], left.pop(0)
        ran[...] = jnp.zeros_like(ran)
        def columns(src, places, dst, sem):
            return [
                pltpu.make_async_copy(
                    src.at[:, pl.ds(pl.multiple_of(ids[place] * depth, depth), depth)],
                    dst.at[:, pl.ds(k * depth, depth)],
                    sem.at[k],
                )
                for k, place in enumerate(places)
            ]

        copies = {n: columns(srcs[n], shards, left[0].at[n], sems.at[n]) for n in range(n_whole)}
        later = [columns(srcs[n_whole + m], some, nexts[m], next_sems.at[m]) for m, (_, some) in enumerate(ahead)]
        if n_whole:
            for copy in copies[0]:
                copy.start()
        else:
            for copy in sum(later, []):
                copy.start()
        for load in loads:
            load.wait()
        first = 0
        for n, (_, some, _) in enumerate(jobs):
            mine = adds[first : first + len(some)]
            first += len(some)
            if whole[n]:
                for copy in copies[n]:
                    copy.wait()
                for copy in copies[n + 1] if n + 1 < n_whole else sum(later, []):
                    copy.start()
                block = left[0].at[n]
            else:
                block = lefts[n]
            for i in range(0, rows, tile):
                span = slice(i, i + tile)
                right = ws[0] if len(ws) == 1 else joined[0]
                result = jnp.dot(block[span, :], right[...], preferred_element_type=jnp.float32)
                for add in mine:
                    result = result + add[span, :].astype(jnp.float32)
                held[n][span, :] = result.astype(outs[n].dtype)
                if last:
                    stores.append(pltpu.make_async_copy(held[n].at[span], outs[n].at[span], out_sems.at[n, i // tile]))
                    stores[-1].start()
        for copy in sum(later, []) + stores:
            copy.wait()

    def result(dtype):
        shape = (rows, cols)
        return pltpu.VMEM(shape, dtype) if dtype == jnp.float32 else jax.ShapeDtypeStruct(shape, dtype)

    aliased = adds
    out_shape = [result(dtype) for _, _, dtype in jobs]
    out_shape += [pltpu.VMEM((rows, len(some) * depth), jnp.bfloat16) for _, some in ahead]
    out_shape += [jax.ShapeDtypeStruct((8, 128), jnp.float32)]
    scratch = [
        pltpu.SemaphoreType.DMA((max(n_whole, 1), count)),
        pltpu.SemaphoreType.DMA((max(len(ahead), 1), wide)),
    ]
    if last:
        scratch += [pltpu.VMEM((rows, cols), jobs[0][2]), pltpu.SemaphoreType.DMA((1, rows // tile))]
    if n_whole:
        scratch.append(pltpu.VMEM((n_whole, rows, count * depth), jnp.bfloat16))
    if len(pieces) > 1:
        scratch += [pltpu.SemaphoreType.DMA((len(pieces),)), pltpu.VMEM((count * depth, cols), jnp.bfloat16)]
    return pl.pallas_call(
        kernel,
        in_specs=[pl.BlockSpec(memory_space=pltpu.SMEM)]
        + [ANY] * (1 + len(sources))
        + [VM] * (len(pieces) + len(laid) + len(adds)),
        out_specs=[ANY if last else VM] * n_jobs + [VM] * (len(out_shape) - n_jobs),
        out_shape=out_shape,
        scratch_shapes=scratch,
        compiler_params=pltpu.CompilerParams(vmem_limit_bytes=16 * 2**20),
        cost_estimate=pl.CostEstimate(flops=flops, bytes_accessed=1000, transcendentals=0),
        input_output_aliases=aliases,
    )(places, after, *[in_hbm(t) for t in sources], *pieces, *laid, *adds)


def in_hbm(value):
    return pltpu.with_memory_space_constraint(value, pltpu.HBM)


def on_device(tokens, weight, momentum, grad, selection):
    rows, cols = weight.shape
    blocks = rows // GROUP
    basis = jnp.asarray(dct_blocks(rows))
    lanes = selection.transpose(0, 2, 3, 1)
    chosen, where = pl.pallas_call(
        coeff_kernel,
        out_shape=(
            jax.ShapeDtypeStruct((blocks, cols), jnp.float32),
            jax.ShapeDtypeStruct((2, 1, 8, cols), jnp.int32),
        ),
        in_specs=[ANY] * 4,
        out_specs=(VM, VM),
        scratch_shapes=[
            pltpu.VMEM((rows, cols), jnp.float32),
            pltpu.VMEM((rows, cols), jnp.float32),
            pltpu.VMEM(lanes.shape[1:], jnp.int32),
            pltpu.VMEM(basis.shape, jnp.float32),
            pltpu.SemaphoreType.DMA((4,)),
        ],
        compiler_params=PARAMS,
        cost_estimate=SMALL,
    )(in_hbm(momentum), in_hbm(grad), in_hbm(lanes), in_hbm(basis))
    along_x = lambda step: lax.ppermute(chosen, "x", [(i, (i + step) % REPS) for i in range(REPS)])
    others = [along_x(k) for k in range(1, REPS)]
    elsewhere = pl.pallas_call(
        functools.partial(others_kernel, blocks),
        out_shape=jax.ShapeDtypeStruct((2, REPS - 1, 8, cols), jnp.int32),
        in_specs=[ANY],
        out_specs=VM,
        scratch_shapes=[pltpu.VMEM((REPS - 1,) + lanes.shape[1:], jnp.int32), pltpu.SemaphoreType.DMA((REPS - 1,))],
        compiler_params=PARAMS,
        cost_estimate=SMALL,
    )(in_hbm(lanes))
    tokens_too = sibling(tokens)
    shard = pl.pallas_call(
        weight_kernel,
        out_shape=jax.ShapeDtypeStruct((rows, cols), jnp.bfloat16),
        in_specs=[VM] * 8,
        out_specs=VM,
        scratch_shapes=[pltpu.VMEM((rows, cols), jnp.float32)],
        compiler_params=PARAMS,
        cost_estimate=SMALL,
    )(weight, chosen, *others, where, elsewhere, basis)

    places = shard_places()
    am, ap = send(shard, "u", 1), send(shard, "u", -1)
    new_momentum = pl.pallas_call(
        momentum_kernel,
        out_shape=jax.ShapeDtypeStruct(momentum.shape, jnp.float32),
        in_specs=[VM] * 4,
        out_specs=VM,
        scratch_shapes=[pltpu.VMEM((rows, cols), jnp.float32)],
        compiler_params=PARAMS,
        cost_estimate=SMALL,
    )(momentum, grad, where, basis)
    am, ap, new_momentum = lax.optimization_barrier((am, ap, new_momentum))
    top, bottom = send(am[: rows // 2], "u", 1), send(ap[rows // 2 :], "u", -1)
    s1 = jnp.concatenate([shard, am], axis=0)
    r1p, r1m = send(s1, "v", 1), send(s1, "v", -1)
    f32, bf16 = jnp.float32, jnp.bfloat16
    second = at((1, 0), (2, 0), (0, -1), (-1, -1), (0, 1), (-1, 1))
    third = at((1, -1), (2, -1), (1, 1), (2, 1))
    near, far = [(0, 2), (-1, 2)], [(1, 2), (2, 2)]
    fourth, fifth, sixth = at(*near), at(*near, other=True) + at(*far), at(*far, other=True)
    mine, theirs, *laid, ran = multiply(
        places,
        [(tokens, (), f32), (tokens_too, (), f32)],
        at((0, 0), (-1, 0)),
        [s1],
        ahead=[(tokens, second), (tokens_too, second)],
        flops=10**10,
    )
    top, bottom, ran = lax.optimization_barrier((top, bottom, ran))
    s2 = jnp.concatenate([ap, top, bottom], axis=0)
    r2p, r2m = send(s2, "v", 1), send(s2, "v", -1)
    f1 = send(r1p, "v", 1)
    mine, theirs, *laid, ran = multiply(
        places,
        [(laid[0], (mine,), f32), (laid[1], (theirs,), f32)],
        second,
        [s2, r1p, r1m],
        ran,
        ahead=[(tokens, third), (tokens_too, third)],
    )
    r2m, ran = lax.optimization_barrier((r2m, ran))
    f2 = send(r2m, "v", -1)
    mine, theirs, *laid, ran = multiply(
        places,
        [(laid[0], (mine,), f32), (laid[1], (theirs,), bf16)],
        third,
        [r2p, r2m],
        ran,
        ahead=[(tokens, some) for some in (fourth, fifth, sixth)],
    )
    theirs = sibling(theirs)
    f1, ran = lax.optimization_barrier((f1, ran))
    g1 = sibling(f1)
    mine, ran = multiply(places, [(laid[0], (mine,), f32)], fourth, [f1], ran)
    f2, ran = lax.optimization_barrier((f2, ran))
    g2 = sibling(f2)
    mine, ran = multiply(places, [(laid[1], (mine,), f32)], fifth, [g1, f2], ran)
    keys, _ = multiply(places, [(laid[2], (mine, theirs), bf16)], sixth, [g2], ran)
    return keys, shard, new_momentum


def solution(mesh):
    chips = Mesh(mesh.devices.reshape(REPS, SIDE, SIDE, 2), ("x",) + PLANE)
    return jax.shard_map(
        on_device,
        mesh=chips,
        in_specs=(
            P(("x",) + PLANE, None),
            P(PLANE, None),
            P("x", PLANE, None),
            P("x", PLANE, None),
            P(),
        ),
        out_specs=(P(("x",) + PLANE, None), P(PLANE, None), P("x", PLANE, None)),
        check_vma=False,
    )
```

```python
import functools

import jax
import jax.numpy as jnp
import numpy as np
from jax import lax
from jax.experimental import pallas as pl
from jax.experimental.pallas import tpu as pltpu
from jax.sharding import Mesh, PartitionSpec as P

GROUP = 64
KEEP = 64
REPS = 4
SIDE = 4
PAIR = 2 * GROUP
PLANE = ("y", "z", "core")

beta_decay = 0.999
step_rate = 0.05

HIGHEST = lax.Precision.HIGHEST
NT = (((1,), (1,)), ((), ()))
TN = (((0,), (0,)), ((), ()))
VM = pl.BlockSpec(memory_space=pltpu.VMEM)
ANY = pl.BlockSpec(memory_space=pl.ANY)
PARAMS = pltpu.CompilerParams(vmem_limit_bytes=32 * 2**20)
ALONE = pltpu.CompilerParams(vmem_limit_bytes=60 * 2**20)
SMALL = pl.CostEstimate(flops=1000, bytes_accessed=1000, transcendentals=0)


def dct_blocks(size):
    freq = np.arange(GROUP, dtype=np.float64)[:, None]
    place = np.arange(GROUP, dtype=np.float64)[None, :]
    scale = np.where(freq == 0, np.sqrt(1.0 / GROUP), np.sqrt(2.0 / GROUP))
    basis = scale * np.cos(np.pi * (2.0 * place + 1.0) * freq / (2.0 * GROUP))
    return np.kron(np.eye(size // GROUP), basis).astype(np.float32)


def halves(value):
    high = value.astype(jnp.bfloat16)
    return high, (value - high.astype(jnp.float32)).astype(jnp.bfloat16)


def dot3(left, right, dims):
    total = None
    for a, b in ((0, 0), (0, 1), (1, 0)):
        part = lax.dot_general(left[a], right[b], dims, preferred_element_type=jnp.float32)
        total = part if total is None else total + part
    return total


def plain(contract):
    return (contract, ((), ()))


def is_row(target, rows):
    return lax.broadcasted_iota(jnp.int32, (rows, target.shape[1]), 0) == target


def one_hot(target, rows):
    return jnp.where(is_row(target, rows), 1.0, 0.0).astype(jnp.bfloat16)


def picker(blocks, lanes):
    first = ((lax.axis_index("y") * SIDE + lax.axis_index("z")) * 2 + lax.axis_index("core")) * blocks
    sub = lax.broadcasted_iota(jnp.int32, (16, 2 * lanes), 0)
    lane = lax.broadcasted_iota(jnp.int32, (16, 2 * lanes), 1)
    mine = jnp.where(sub < 8, first + sub, lanes + first + sub - 8)
    return jnp.where((lane == mine) & (jnp.bitwise_and(sub, 7) < blocks), 1.0, 0.0).astype(jnp.bfloat16)


def place_of(flat, pick, where, r):
    cols, lanes = flat.shape[0] * flat.shape[1], flat.shape[2]
    flat = flat.reshape(cols, lanes)
    row = jnp.right_shift(flat, 6).astype(jnp.float32).astype(jnp.bfloat16)
    col = jnp.bitwise_and(flat, GROUP - 1).astype(jnp.float32).astype(jnp.bfloat16)
    both = lax.dot_general(pick, jnp.concatenate([row, col], axis=1), NT, preferred_element_type=jnp.float32)
    both = both.astype(jnp.int32)
    where[0, r] = both[:8]
    where[1, r] = both[8:] + jnp.bitwise_and(lax.broadcasted_iota(jnp.int32, (8, cols), 1), GROUP)


def coeff_kernel(momentum, grad, selection, basis, chosen, where, mom, gra, sel, dct, sems):
    blocks = mom.shape[0] // GROUP
    copies = [
        pltpu.make_async_copy(selection.at[lax.axis_index("x")], sel, sems.at[0]),
        pltpu.make_async_copy(momentum.at[0], mom, sems.at[1]),
        pltpu.make_async_copy(grad.at[0], gra, sems.at[2]),
        pltpu.make_async_copy(basis, dct, sems.at[3]),
    ]
    for copy in copies:
        copy.start()
    pick = picker(blocks, sel.shape[2])
    copies[0].wait()
    place_of(sel[...], pick, where, 0)
    for copy in copies[1:]:
        copy.wait()
    base = halves(dct[...])
    moment = halves(beta_decay * mom[...] + gra[...])
    inner = halves(dot3(base, moment, plain(((1,), (0,)))))
    width = base[0].shape[0]
    for c in range(0, mom.shape[1], width):
        coeff = dot3([part[:, c : c + width] for part in inner], base, NT)
        high, low = halves(coeff)
        for p in range(c, c + width, PAIR):
            span = slice(p - c, p - c + PAIR)
            for a in range(blocks):
                rows = slice(a * GROUP, (a + 1) * GROUP)
                left = jnp.concatenate([high[rows, span], low[rows, span]], axis=1)
                right = one_hot(where[1, 0, a : a + 1, p : p + PAIR], PAIR)
                found = jnp.dot(left, jnp.concatenate([right, right], axis=0), preferred_element_type=jnp.float32)
                kept = jnp.where(is_row(where[0, 0, a : a + 1, p : p + PAIR], GROUP), found, 0.0)
                chosen[a : a + 1, p : p + PAIR] = jnp.sum(kept, axis=0, keepdims=True)


def others_kernel(blocks, selection, where, sel, sems):
    copies = []
    for k in range(REPS - 1):
        r = lax.rem(lax.axis_index("x") + REPS - 1 - k, REPS)
        copies.append(pltpu.make_async_copy(selection.at[r], sel.at[k], sems.at[k]))
        copies[-1].start()
    pick = picker(blocks, sel.shape[3])
    for k in range(REPS - 1):
        copies[k].wait()
        place_of(sel[k], pick, where, k)


def weight_kernel(weight, chosen0, chosen1, chosen2, chosen3, where, others, basis, new_weight, dense):
    rows, cols = weight.shape
    base = halves(basis[...])
    blocks = rows // GROUP
    kinds = [[], [], [], []]
    for k, chosen in enumerate((chosen0, chosen1, chosen2, chosen3)):
        places, r = (others, k - 1) if k else (where, 0)
        high, low = halves(chosen[...])
        kinds[0].append(places[0, r][:blocks])
        kinds[1].append(jnp.bitwise_and(places[1, r][:blocks], GROUP - 1))
        kinds[2].append(high.astype(jnp.float32))
        kinds[3].append(low.astype(jnp.float32))
    lane = lax.broadcasted_iota(jnp.int32, (GROUP, PAIR), 1)
    for p in range(0, cols, PAIR):
        sides = []
        for at in (p, p + GROUP):
            sides.append([jnp.concatenate([x[:, at : at + KEEP] for x in kind], axis=1) for kind in kinds])
        for a in range(blocks):
            sums = []
            for row, col, high, low in sides:
                left = one_hot(row[a : a + 1], GROUP)
                hit = is_row(col[a : a + 1], GROUP)
                right = [jnp.where(hit, x[a : a + 1], 0.0).astype(jnp.bfloat16) for x in (high, low)]
                both = lax.dot_general(left, jnp.concatenate(right, axis=0), NT, preferred_element_type=jnp.float32)
                sums.append(both + pltpu.roll(both, GROUP, 1))
            dense[a * GROUP : (a + 1) * GROUP, p : p + PAIR] = jnp.where(lane < GROUP, *sums)
    inner = halves(dot3(base, halves(dense[...]), TN))
    width = rows
    for c in range(0, cols, width):
        update = dot3([part[:, c : c + width] for part in inner], base, plain(((1,), (0,))))
        old = weight[:, c : c + width].astype(jnp.float32)
        new_weight[:, c : c + width] = (old - step_rate * update).astype(jnp.bfloat16)


def momentum_kernel(momentum, grad, where, basis, new_momentum, dense):
    rows, cols = dense.shape
    base = basis[...]
    moment = beta_decay * momentum[0] + grad[0]
    inner = jnp.dot(base, moment, precision=HIGHEST, preferred_element_type=jnp.float32)
    width = rows
    for c in range(0, cols, width):
        coeff = lax.dot_general(inner[:, c : c + width], base, NT, precision=HIGHEST, preferred_element_type=jnp.float32)
        for p in range(c, c + width, PAIR):
            for a in range(rows // GROUP):
                left = one_hot(where[0, 0, a : a + 1, p : p + PAIR], GROUP)
                right = one_hot(where[1, 0, a : a + 1, p : p + PAIR], PAIR)
                kept = lax.dot_general(left, right, NT, preferred_element_type=jnp.float32)
                span = slice(a * GROUP, (a + 1) * GROUP)
                dense[span, p : p + PAIR] = jnp.where(kept > 0.5, coeff[span, p - c : p - c + PAIR], 0.0)
    inner = lax.dot_general(base, dense[...], TN, precision=HIGHEST, preferred_element_type=jnp.float32)
    for c in range(0, cols, width):
        own_part = jnp.dot(inner[:, c : c + width], base, precision=HIGHEST, preferred_element_type=jnp.float32)
        moment = beta_decay * momentum[0, :, c : c + width] + grad[0, :, c : c + width]
        new_momentum[0, :, c : c + width] = moment - own_part


def ring(axis, step):
    pairs = []
    for y in range(SIDE):
        for z in range(SIDE):
            for c in range(2):
                if (c == 0) == (axis == "u"):
                    to = ((y + step) % SIDE, z)
                else:
                    to = (y, (z + step) % SIDE)
                pairs.append(((y * SIDE + z) * 2 + c, (to[0] * SIDE + to[1]) * 2 + c))
    return pairs


def send(value, axis, step):
    return lax.ppermute(value, PLANE, ring(axis, step))


def sibling(value):
    return lax.ppermute(value, "core", [(0, 1), (1, 0)])


def shard_places():
    y, z, c = lax.axis_index("y"), lax.axis_index("z"), lax.axis_index("core")
    k = np.arange(2 * SIDE * SIDE)
    u, v = jnp.asarray(k // SIDE % SIDE, jnp.int32), jnp.asarray(k % SIDE, jnp.int32)
    core = jnp.where(jnp.asarray(k < SIDE * SIDE), c, 1 - c)
    even = jnp.bitwise_and(y + u, 3) * SIDE + jnp.bitwise_and(z + v, 3)
    odd = jnp.bitwise_and(y + v, 3) * SIDE + jnp.bitwise_and(z + u, 3)
    return 2 * jnp.where(core == 0, even, odd) + core


def at(*offsets, other=False):
    return [(u % SIDE) * SIDE + v % SIDE + (SIDE * SIDE if other else 0) for u, v in offsets]


def multiply(places, jobs, shards, pieces, after=None, ahead=(), last=False, flops=1000):
    depth, tile = 256, 256
    rows, cols, count = jobs[0][0].shape[0], pieces[0].shape[1], len(shards)
    whole = [tok.shape[1] > count * depth for tok, _, _ in jobs]
    sources = [tok for (tok, _, _), w in zip(jobs, whole) if w] + [tok for tok, _ in ahead]
    laid = [tok for (tok, _, _), w in zip(jobs, whole) if not w]
    adds = [x for _, some, _ in jobs for x in some]
    n_jobs, n_whole = len(jobs), sum(whole)
    wide = max([len(some) for _, some in ahead], default=1)
    after = jnp.zeros((8, 128), jnp.float32) if after is None else after
    aliases, at = {}, 2 + len(sources) + len(pieces) + len(laid)
    for n, (_, some, dtype) in enumerate(jobs):
        if some and some[0].dtype == dtype:
            aliases[at] = n
        at += len(some)

    def kernel(ids, _, *refs):
        refs = list(refs)
        take = lambda n: [refs.pop(0) for _ in range(n)]
        srcs, ws, lefts, adds = take(len(sources)), take(len(pieces)), take(len(laid)), take(len(aliased))
        outs, nexts, (ran, *scratch) = take(n_jobs), take(len(ahead)), refs
        sems, next_sems, *left = scratch
        joined, loads, at = [], [], 0
        if len(ws) > 1:
            joined, piece_sems = [left.pop()], left.pop()
            for k, w in enumerate(ws):
                loads.append(pltpu.make_async_copy(w, joined[0].at[pl.ds(at, w.shape[0])], piece_sems.at[k]))
                loads[-1].start()
                at += w.shape[0]
        held, stores = outs, []
        if last:
            held, out_sems = [left.pop(0)], left.pop(0)
        ran[...] = jnp.zeros_like(ran)
        def columns(src, places, dst, sem):
            return [
                pltpu.make_async_copy(
                    src.at[:, pl.ds(pl.multiple_of(ids[place] * depth, depth), depth)],
                    dst.at[:, pl.ds(k * depth, depth)],
                    sem.at[k],
                )
                for k, place in enumerate(places)
            ]

        copies = {n: columns(srcs[n], shards, left[0].at[n], sems.at[n]) for n in range(n_whole)}
        later = [columns(srcs[n_whole + m], some, nexts[m], next_sems.at[m]) for m, (_, some) in enumerate(ahead)]
        if n_whole:
            for copy in copies[0]:
                copy.start()
        else:
            for copy in sum(later, []):
                copy.start()
        for load in loads:
            load.wait()
        first = 0
        for n, (_, some, _) in enumerate(jobs):
            mine = adds[first : first + len(some)]
            first += len(some)
            if whole[n]:
                for copy in copies[n]:
                    copy.wait()
                for copy in copies[n + 1] if n + 1 < n_whole else sum(later, []):
                    copy.start()
                block = left[0].at[n]
            else:
                block = lefts[n]
            for i in range(0, rows, tile):
                span = slice(i, i + tile)
                right = ws[0] if len(ws) == 1 else joined[0]
                result = jnp.dot(block[span, :], right[...], preferred_element_type=jnp.float32)
                for add in mine:
                    result = result + add[span, :].astype(jnp.float32)
                held[n][span, :] = result.astype(outs[n].dtype)
                if last:
                    stores.append(pltpu.make_async_copy(held[n].at[span], outs[n].at[span], out_sems.at[n, i // tile]))
                    stores[-1].start()
        for copy in sum(later, []) + stores:
            copy.wait()

    def result(dtype):
        shape = (rows, cols)
        return pltpu.VMEM(shape, dtype) if dtype == jnp.float32 else jax.ShapeDtypeStruct(shape, dtype)

    aliased = adds
    out_shape = [result(dtype) for _, _, dtype in jobs]
    out_shape += [pltpu.VMEM((rows, len(some) * depth), jnp.bfloat16) for _, some in ahead]
    out_shape += [jax.ShapeDtypeStruct((8, 128), jnp.float32)]
    scratch = [
        pltpu.SemaphoreType.DMA((max(n_whole, 1), count)),
        pltpu.SemaphoreType.DMA((max(len(ahead), 1), wide)),
    ]
    if last:
        scratch += [pltpu.VMEM((rows, cols), jobs[0][2]), pltpu.SemaphoreType.DMA((1, rows // tile))]
    if n_whole:
        scratch.append(pltpu.VMEM((n_whole, rows, count * depth), jnp.bfloat16))
    if len(pieces) > 1:
        scratch += [pltpu.SemaphoreType.DMA((len(pieces),)), pltpu.VMEM((count * depth, cols), jnp.bfloat16)]
    return pl.pallas_call(
        kernel,
        in_specs=[pl.BlockSpec(memory_space=pltpu.SMEM)]
        + [ANY] * (1 + len(sources))
        + [VM] * (len(pieces) + len(laid) + len(adds)),
        out_specs=[ANY if last else VM] * n_jobs + [VM] * (len(out_shape) - n_jobs),
        out_shape=out_shape,
        scratch_shapes=scratch,
        compiler_params=pltpu.CompilerParams(vmem_limit_bytes=16 * 2**20),
        cost_estimate=pl.CostEstimate(flops=flops, bytes_accessed=1000, transcendentals=0),
        input_output_aliases=aliases,
    )(places, after, *[in_hbm(t) for t in sources], *pieces, *laid, *adds)


def in_hbm(value):
    return pltpu.with_memory_space_constraint(value, pltpu.HBM)


def on_device(tokens, weight, momentum, grad, selection):
    rows, cols = weight.shape
    blocks = rows // GROUP
    basis = jnp.asarray(dct_blocks(rows))
    lanes = selection.transpose(0, 2, 3, 1)
    chosen, where = pl.pallas_call(
        coeff_kernel,
        out_shape=(
            jax.ShapeDtypeStruct((blocks, cols), jnp.float32),
            jax.ShapeDtypeStruct((2, 1, 8, cols), jnp.int32),
        ),
        in_specs=[ANY] * 4,
        out_specs=(VM, VM),
        scratch_shapes=[
            pltpu.VMEM((rows, cols), jnp.float32),
            pltpu.VMEM((rows, cols), jnp.float32),
            pltpu.VMEM(lanes.shape[1:], jnp.int32),
            pltpu.VMEM(basis.shape, jnp.float32),
            pltpu.SemaphoreType.DMA((4,)),
        ],
        compiler_params=PARAMS,
        cost_estimate=SMALL,
    )(in_hbm(momentum), in_hbm(grad), in_hbm(lanes), in_hbm(basis))
    along_x = lambda step: lax.ppermute(chosen, "x", [(i, (i + step) % REPS) for i in range(REPS)])
    others = [along_x(k) for k in range(1, REPS)]
    elsewhere = pl.pallas_call(
        functools.partial(others_kernel, blocks),
        out_shape=jax.ShapeDtypeStruct((2, REPS - 1, 8, cols), jnp.int32),
        in_specs=[ANY],
        out_specs=VM,
        scratch_shapes=[pltpu.VMEM((REPS - 1,) + lanes.shape[1:], jnp.int32), pltpu.SemaphoreType.DMA((REPS - 1,))],
        compiler_params=PARAMS,
        cost_estimate=SMALL,
    )(in_hbm(lanes))
    tokens_too = sibling(tokens)
    shard = pl.pallas_call(
        weight_kernel,
        out_shape=jax.ShapeDtypeStruct((rows, cols), jnp.bfloat16),
        in_specs=[VM] * 8,
        out_specs=VM,
        scratch_shapes=[pltpu.VMEM((rows, cols), jnp.float32)],
        compiler_params=PARAMS,
        cost_estimate=SMALL,
    )(weight, chosen, *others, where, elsewhere, basis)

    places = shard_places()
    am, ap = send(shard, "u", 1), send(shard, "u", -1)
    new_momentum = pl.pallas_call(
        momentum_kernel,
        out_shape=jax.ShapeDtypeStruct(momentum.shape, jnp.float32),
        in_specs=[VM] * 4,
        out_specs=VM,
        scratch_shapes=[pltpu.VMEM((rows, cols), jnp.float32)],
        compiler_params=PARAMS,
        cost_estimate=SMALL,
    )(momentum, grad, where, basis)
    am, ap, new_momentum = lax.optimization_barrier((am, ap, new_momentum))
    top, bottom = send(am[: rows // 2], "u", 1), send(ap[rows // 2 :], "u", -1)
    s1 = jnp.concatenate([shard, am], axis=0)
    r1p, r1m = send(s1, "v", 1), send(s1, "v", -1)
    f32, bf16 = jnp.float32, jnp.bfloat16
    second = at((1, 0), (2, 0), (0, -1), (-1, -1), (0, 1), (-1, 1))
    third = at((1, -1), (2, -1), (1, 1), (2, 1))
    near, far = [(0, 2), (-1, 2)], [(1, 2), (2, 2)]
    fourth, fifth, sixth = at(*near), at(*near, other=True) + at(*far), at(*far, other=True)
    mine, theirs, *laid, ran = multiply(
        places,
        [(tokens, (), f32), (tokens_too, (), f32)],
        at((0, 0), (-1, 0)),
        [s1],
        ahead=[(tokens, second), (tokens_too, second)],
        flops=10**10,
    )
    top, bottom, ran = lax.optimization_barrier((top, bottom, ran))
    s2 = jnp.concatenate([ap, top, bottom], axis=0)
    r2p, r2m = send(s2, "v", 1), send(s2, "v", -1)
    f1 = send(r1p, "v", 1)
    mine, theirs, *laid, ran = multiply(
        places,
        [(laid[0], (mine,), f32), (laid[1], (theirs,), f32)],
        second,
        [s2, r1p, r1m],
        ran,
        ahead=[(tokens, third), (tokens_too, third)],
    )
    r2m, ran = lax.optimization_barrier((r2m, ran))
    f2 = send(r2m, "v", -1)
    mine, theirs, *laid, ran = multiply(
        places,
        [(laid[0], (mine,), f32), (laid[1], (theirs,), bf16)],
        third,
        [r2p, r2m],
        ran,
        ahead=[(tokens, some) for some in (fourth, fifth, sixth)],
    )
    theirs = sibling(theirs)
    f1, ran = lax.optimization_barrier((f1, ran))
    g1 = sibling(f1)
    mine, ran = multiply(places, [(laid[0], (mine,), f32)], fourth, [f1], ran)
    f2, ran = lax.optimization_barrier((f2, ran))
    g2 = sibling(f2)
    mine, ran = multiply(places, [(laid[1], (mine,), f32)], fifth, [g1, f2], ran)
    keys, _ = multiply(places, [(laid[2], (mine, theirs), bf16)], sixth, [g2], ran)
    return keys, shard, new_momentum


def solution(mesh):
    chips = Mesh(mesh.devices.reshape(REPS, SIDE, SIDE, 2), ("x",) + PLANE)
    return jax.shard_map(
        on_device,
        mesh=chips,
        in_specs=(
            P(("x",) + PLANE, None),
            P(PLANE, None),
            P("x", PLANE, None),
            P("x", PLANE, None),
            P(),
        ),
        out_specs=(P(("x",) + PLANE, None), P(PLANE, None), P("x", PLANE, None)),
        check_vma=False,
    )
```

```python
import functools

import jax
import jax.numpy as jnp
import numpy as np
from jax import lax
from jax.experimental import pallas as pl
from jax.experimental.pallas import tpu as pltpu
from jax.sharding import Mesh, PartitionSpec as P

GROUP = 64
KEEP = 64
REPS = 4
SIDE = 4
PAIR = 2 * GROUP
PLANE = ("y", "z", "core")

beta_decay = 0.999
step_rate = 0.05

HIGHEST = lax.Precision.HIGHEST
NT = (((1,), (1,)), ((), ()))
TN = (((0,), (0,)), ((), ()))
VM = pl.BlockSpec(memory_space=pltpu.VMEM)
ANY = pl.BlockSpec(memory_space=pl.ANY)
PARAMS = pltpu.CompilerParams(vmem_limit_bytes=32 * 2**20)
ALONE = pltpu.CompilerParams(vmem_limit_bytes=60 * 2**20)
SMALL = pl.CostEstimate(flops=1000, bytes_accessed=1000, transcendentals=0)


def dct_blocks(size):
    freq = np.arange(GROUP, dtype=np.float64)[:, None]
    place = np.arange(GROUP, dtype=np.float64)[None, :]
    scale = np.where(freq == 0, np.sqrt(1.0 / GROUP), np.sqrt(2.0 / GROUP))
    basis = scale * np.cos(np.pi * (2.0 * place + 1.0) * freq / (2.0 * GROUP))
    return np.kron(np.eye(size // GROUP), basis).astype(np.float32)


def halves(value):
    high = value.astype(jnp.bfloat16)
    return high, (value - high.astype(jnp.float32)).astype(jnp.bfloat16)


def dot3(left, right, dims):
    total = None
    for a, b in ((0, 0), (0, 1), (1, 0)):
        part = lax.dot_general(left[a], right[b], dims, preferred_element_type=jnp.float32)
        total = part if total is None else total + part
    return total


def plain(contract):
    return (contract, ((), ()))


def is_row(target, rows):
    return lax.broadcasted_iota(jnp.int32, (rows, target.shape[1]), 0) == target


def one_hot(target, rows):
    return jnp.where(is_row(target, rows), 1.0, 0.0).astype(jnp.bfloat16)


def picker(blocks, lanes):
    first = ((lax.axis_index("y") * SIDE + lax.axis_index("z")) * 2 + lax.axis_index("core")) * blocks
    sub = lax.broadcasted_iota(jnp.int32, (16, 2 * lanes), 0)
    lane = lax.broadcasted_iota(jnp.int32, (16, 2 * lanes), 1)
    mine = jnp.where(sub < 8, first + sub, lanes + first + sub - 8)
    return jnp.where((lane == mine) & (jnp.bitwise_and(sub, 7) < blocks), 1.0, 0.0).astype(jnp.bfloat16)


def place_of(flat, pick, where, r):
    cols, lanes = flat.shape[0] * flat.shape[1], flat.shape[2]
    flat = flat.reshape(cols, lanes)
    row = jnp.right_shift(flat, 6).astype(jnp.float32).astype(jnp.bfloat16)
    col = jnp.bitwise_and(flat, GROUP - 1).astype(jnp.float32).astype(jnp.bfloat16)
    both = lax.dot_general(pick, jnp.concatenate([row, col], axis=1), NT, preferred_element_type=jnp.float32)
    both = both.astype(jnp.int32)
    where[0, r] = both[:8]
    where[1, r] = both[8:] + jnp.bitwise_and(lax.broadcasted_iota(jnp.int32, (8, cols), 1), GROUP)


def coeff_kernel(momentum, grad, selection, basis, chosen, where, mom, gra, sel, dct, sems):
    blocks = mom.shape[0] // GROUP
    copies = [
        pltpu.make_async_copy(selection.at[lax.axis_index("x")], sel, sems.at[0]),
        pltpu.make_async_copy(momentum.at[0], mom, sems.at[1]),
        pltpu.make_async_copy(grad.at[0], gra, sems.at[2]),
        pltpu.make_async_copy(basis, dct, sems.at[3]),
    ]
    for copy in copies:
        copy.start()
    pick = picker(blocks, sel.shape[2])
    copies[0].wait()
    place_of(sel[...], pick, where, 0)
    for copy in copies[1:]:
        copy.wait()
    base = halves(dct[...])
    moment = halves(beta_decay * mom[...] + gra[...])
    inner = halves(dot3(base, moment, plain(((1,), (0,)))))
    width = base[0].shape[0]
    for c in range(0, mom.shape[1], width):
        coeff = dot3([part[:, c : c + width] for part in inner], base, NT)
        high, low = halves(coeff)
        for p in range(c, c + width, PAIR):
            span = slice(p - c, p - c + PAIR)
            for a in range(blocks):
                rows = slice(a * GROUP, (a + 1) * GROUP)
                left = jnp.concatenate([high[rows, span], low[rows, span]], axis=0)
                right = one_hot(where[1, 0, a : a + 1, p : p + PAIR], PAIR)
                found = jnp.dot(left, right, preferred_element_type=jnp.float32)
                found = found[:GROUP] + found[GROUP:]
                kept = jnp.where(is_row(where[0, 0, a : a + 1, p : p + PAIR], GROUP), found, 0.0)
                chosen[a : a + 1, p : p + PAIR] = jnp.sum(kept, axis=0, keepdims=True)


def others_kernel(blocks, selection, where, sel, sems):
    copies = []
    for k in range(REPS - 1):
        r = lax.rem(lax.axis_index("x") + REPS - 1 - k, REPS)
        copies.append(pltpu.make_async_copy(selection.at[r], sel.at[k], sems.at[k]))
        copies[-1].start()
    pick = picker(blocks, sel.shape[3])
    for k in range(REPS - 1):
        copies[k].wait()
        place_of(sel[k], pick, where, k)


def weight_kernel(weight, chosen0, chosen1, chosen2, chosen3, where, others, basis, new_weight, dense):
    rows, cols = weight.shape
    base = halves(basis[...])
    blocks = rows // GROUP
    kinds = [[], [], [], []]
    for k, chosen in enumerate((chosen0, chosen1, chosen2, chosen3)):
        places, r = (others, k - 1) if k else (where, 0)
        high, low = halves(chosen[...])
        kinds[0].append(places[0, r][:blocks])
        kinds[1].append(jnp.bitwise_and(places[1, r][:blocks], GROUP - 1))
        kinds[2].append(high.astype(jnp.float32))
        kinds[3].append(low.astype(jnp.float32))
    lane = lax.broadcasted_iota(jnp.int32, (GROUP, PAIR), 1)
    for p in range(0, cols, PAIR):
        sides = []
        for at in (p, p + GROUP):
            sides.append([jnp.concatenate([x[:, at : at + KEEP] for x in kind], axis=1) for kind in kinds])
        for a in range(blocks):
            sums = []
            for row, col, high, low in sides:
                left = one_hot(row[a : a + 1], GROUP)
                hit = is_row(col[a : a + 1], GROUP)
                right = [jnp.where(hit, x[a : a + 1], 0.0).astype(jnp.bfloat16) for x in (high, low)]
                both = lax.dot_general(left, jnp.concatenate(right, axis=0), NT, preferred_element_type=jnp.float32)
                sums.append(both + pltpu.roll(both, GROUP, 1))
            dense[a * GROUP : (a + 1) * GROUP, p : p + PAIR] = jnp.where(lane < GROUP, *sums)
    inner = halves(dot3(base, halves(dense[...]), TN))
    width = rows
    for c in range(0, cols, width):
        update = dot3([part[:, c : c + width] for part in inner], base, plain(((1,), (0,))))
        old = weight[:, c : c + width].astype(jnp.float32)
        new_weight[:, c : c + width] = (old - step_rate * update).astype(jnp.bfloat16)


def momentum_kernel(momentum, grad, where, basis, new_momentum, dense):
    rows, cols = dense.shape
    base = basis[...]
    moment = beta_decay * momentum[0] + grad[0]
    inner = jnp.dot(base, moment, precision=HIGHEST, preferred_element_type=jnp.float32)
    width = rows
    for c in range(0, cols, width):
        coeff = lax.dot_general(inner[:, c : c + width], base, NT, precision=HIGHEST, preferred_element_type=jnp.float32)
        for p in range(c, c + width, PAIR):
            for a in range(rows // GROUP):
                left = one_hot(where[0, 0, a : a + 1, p : p + PAIR], GROUP)
                right = one_hot(where[1, 0, a : a + 1, p : p + PAIR], PAIR)
                kept = lax.dot_general(left, right, NT, preferred_element_type=jnp.float32)
                span = slice(a * GROUP, (a + 1) * GROUP)
                dense[span, p : p + PAIR] = jnp.where(kept > 0.5, coeff[span, p - c : p - c + PAIR], 0.0)
    inner = lax.dot_general(base, dense[...], TN, precision=HIGHEST, preferred_element_type=jnp.float32)
    for c in range(0, cols, width):
        own_part = jnp.dot(inner[:, c : c + width], base, precision=HIGHEST, preferred_element_type=jnp.float32)
        moment = beta_decay * momentum[0, :, c : c + width] + grad[0, :, c : c + width]
        new_momentum[0, :, c : c + width] = moment - own_part


def ring(axis, step):
    pairs = []
    for y in range(SIDE):
        for z in range(SIDE):
            for c in range(2):
                if (c == 0) == (axis == "u"):
                    to = ((y + step) % SIDE, z)
                else:
                    to = (y, (z + step) % SIDE)
                pairs.append(((y * SIDE + z) * 2 + c, (to[0] * SIDE + to[1]) * 2 + c))
    return pairs


def send(value, axis, step):
    return lax.ppermute(value, PLANE, ring(axis, step))


def sibling(value):
    return lax.ppermute(value, "core", [(0, 1), (1, 0)])


def shard_places():
    y, z, c = lax.axis_index("y"), lax.axis_index("z"), lax.axis_index("core")
    k = np.arange(2 * SIDE * SIDE)
    u, v = jnp.asarray(k // SIDE % SIDE, jnp.int32), jnp.asarray(k % SIDE, jnp.int32)
    core = jnp.where(jnp.asarray(k < SIDE * SIDE), c, 1 - c)
    even = jnp.bitwise_and(y + u, 3) * SIDE + jnp.bitwise_and(z + v, 3)
    odd = jnp.bitwise_and(y + v, 3) * SIDE + jnp.bitwise_and(z + u, 3)
    return 2 * jnp.where(core == 0, even, odd) + core


def at(*offsets, other=False):
    return [(u % SIDE) * SIDE + v % SIDE + (SIDE * SIDE if other else 0) for u, v in offsets]


def multiply(places, jobs, shards, pieces, after=None, ahead=(), last=False, flops=1000):
    depth, tile = 256, 256
    rows, cols, count = jobs[0][0].shape[0], pieces[0].shape[1], len(shards)
    whole = [tok.shape[1] > count * depth for tok, _, _ in jobs]
    sources = [tok for (tok, _, _), w in zip(jobs, whole) if w] + [tok for tok, _ in ahead]
    laid = [tok for (tok, _, _), w in zip(jobs, whole) if not w]
    adds = [x for _, some, _ in jobs for x in some]
    n_jobs, n_whole = len(jobs), sum(whole)
    wide = max([len(some) for _, some in ahead], default=1)
    after = jnp.zeros((8, 128), jnp.float32) if after is None else after
    aliases, at = {}, 2 + len(sources) + len(pieces) + len(laid)
    for n, (_, some, dtype) in enumerate(jobs):
        if some and some[0].dtype == dtype:
            aliases[at] = n
        at += len(some)

    def kernel(ids, _, *refs):
        refs = list(refs)
        take = lambda n: [refs.pop(0) for _ in range(n)]
        srcs, ws, lefts, adds = take(len(sources)), take(len(pieces)), take(len(laid)), take(len(aliased))
        outs, nexts, (ran, *scratch) = take(n_jobs), take(len(ahead)), refs
        sems, next_sems, *left = scratch
        joined, loads, at = [], [], 0
        if len(ws) > 1:
            joined, piece_sems = [left.pop()], left.pop()
            for k, w in enumerate(ws):
                loads.append(pltpu.make_async_copy(w, joined[0].at[pl.ds(at, w.shape[0])], piece_sems.at[k]))
                loads[-1].start()
                at += w.shape[0]
        held, stores = outs, []
        if last:
            held, out_sems = [left.pop(0)], left.pop(0)
        ran[...] = jnp.zeros_like(ran)
        def columns(src, places, dst, sem):
            return [
                pltpu.make_async_copy(
                    src.at[:, pl.ds(pl.multiple_of(ids[place] * depth, depth), depth)],
                    dst.at[:, pl.ds(k * depth, depth)],
                    sem.at[k],
                )
                for k, place in enumerate(places)
            ]

        copies = {n: columns(srcs[n], shards, left[0].at[n], sems.at[n]) for n in range(n_whole)}
        later = [columns(srcs[n_whole + m], some, nexts[m], next_sems.at[m]) for m, (_, some) in enumerate(ahead)]
        if n_whole:
            for copy in copies[0]:
                copy.start()
        else:
            for copy in sum(later, []):
                copy.start()
        for load in loads:
            load.wait()
        first = 0
        for n, (_, some, _) in enumerate(jobs):
            mine = adds[first : first + len(some)]
            first += len(some)
            if whole[n]:
                for copy in copies[n]:
                    copy.wait()
                for copy in copies[n + 1] if n + 1 < n_whole else sum(later, []):
                    copy.start()
                block = left[0].at[n]
            else:
                block = lefts[n]
            for i in range(0, rows, tile):
                span = slice(i, i + tile)
                right = ws[0] if len(ws) == 1 else joined[0]
                result = jnp.dot(block[span, :], right[...], preferred_element_type=jnp.float32)
                for add in mine:
                    result = result + add[span, :].astype(jnp.float32)
                held[n][span, :] = result.astype(outs[n].dtype)
                if last:
                    stores.append(pltpu.make_async_copy(held[n].at[span], outs[n].at[span], out_sems.at[n, i // tile]))
                    stores[-1].start()
        for copy in sum(later, []) + stores:
            copy.wait()

    def result(dtype):
        shape = (rows, cols)
        return pltpu.VMEM(shape, dtype) if dtype == jnp.float32 else jax.ShapeDtypeStruct(shape, dtype)

    aliased = adds
    out_shape = [result(dtype) for _, _, dtype in jobs]
    out_shape += [pltpu.VMEM((rows, len(some) * depth), jnp.bfloat16) for _, some in ahead]
    out_shape += [jax.ShapeDtypeStruct((8, 128), jnp.float32)]
    scratch = [
        pltpu.SemaphoreType.DMA((max(n_whole, 1), count)),
        pltpu.SemaphoreType.DMA((max(len(ahead), 1), wide)),
    ]
    if last:
        scratch += [pltpu.VMEM((rows, cols), jobs[0][2]), pltpu.SemaphoreType.DMA((1, rows // tile))]
    if n_whole:
        scratch.append(pltpu.VMEM((n_whole, rows, count * depth), jnp.bfloat16))
    if len(pieces) > 1:
        scratch += [pltpu.SemaphoreType.DMA((len(pieces),)), pltpu.VMEM((count * depth, cols), jnp.bfloat16)]
    return pl.pallas_call(
        kernel,
        in_specs=[pl.BlockSpec(memory_space=pltpu.SMEM)]
        + [ANY] * (1 + len(sources))
        + [VM] * (len(pieces) + len(laid) + len(adds)),
        out_specs=[ANY if last else VM] * n_jobs + [VM] * (len(out_shape) - n_jobs),
        out_shape=out_shape,
        scratch_shapes=scratch,
        compiler_params=pltpu.CompilerParams(vmem_limit_bytes=16 * 2**20),
        cost_estimate=pl.CostEstimate(flops=flops, bytes_accessed=1000, transcendentals=0),
        input_output_aliases=aliases,
    )(places, after, *[in_hbm(t) for t in sources], *pieces, *laid, *adds)


def in_hbm(value):
    return pltpu.with_memory_space_constraint(value, pltpu.HBM)


def on_device(tokens, weight, momentum, grad, selection):
    rows, cols = weight.shape
    blocks = rows // GROUP
    basis = jnp.asarray(dct_blocks(rows))
    lanes = selection.transpose(0, 2, 3, 1)
    chosen, where = pl.pallas_call(
        coeff_kernel,
        out_shape=(
            jax.ShapeDtypeStruct((blocks, cols), jnp.float32),
            jax.ShapeDtypeStruct((2, 1, 8, cols), jnp.int32),
        ),
        in_specs=[ANY] * 4,
        out_specs=(VM, VM),
        scratch_shapes=[
            pltpu.VMEM((rows, cols), jnp.float32),
            pltpu.VMEM((rows, cols), jnp.float32),
            pltpu.VMEM(lanes.shape[1:], jnp.int32),
            pltpu.VMEM(basis.shape, jnp.float32),
            pltpu.SemaphoreType.DMA((4,)),
        ],
        compiler_params=PARAMS,
        cost_estimate=SMALL,
    )(in_hbm(momentum), in_hbm(grad), in_hbm(lanes), in_hbm(basis))
    along_x = lambda step: lax.ppermute(chosen, "x", [(i, (i + step) % REPS) for i in range(REPS)])
    others = [along_x(k) for k in range(1, REPS)]
    elsewhere = pl.pallas_call(
        functools.partial(others_kernel, blocks),
        out_shape=jax.ShapeDtypeStruct((2, REPS - 1, 8, cols), jnp.int32),
        in_specs=[ANY],
        out_specs=VM,
        scratch_shapes=[pltpu.VMEM((REPS - 1,) + lanes.shape[1:], jnp.int32), pltpu.SemaphoreType.DMA((REPS - 1,))],
        compiler_params=PARAMS,
        cost_estimate=SMALL,
    )(in_hbm(lanes))
    tokens_too = sibling(tokens)
    shard = pl.pallas_call(
        weight_kernel,
        out_shape=jax.ShapeDtypeStruct((rows, cols), jnp.bfloat16),
        in_specs=[VM] * 8,
        out_specs=VM,
        scratch_shapes=[pltpu.VMEM((rows, cols), jnp.float32)],
        compiler_params=PARAMS,
        cost_estimate=SMALL,
    )(weight, chosen, *others, where, elsewhere, basis)

    places = shard_places()
    am, ap = send(shard, "u", 1), send(shard, "u", -1)
    new_momentum = pl.pallas_call(
        momentum_kernel,
        out_shape=jax.ShapeDtypeStruct(momentum.shape, jnp.float32),
        in_specs=[VM] * 4,
        out_specs=VM,
        scratch_shapes=[pltpu.VMEM((rows, cols), jnp.float32)],
        compiler_params=PARAMS,
        cost_estimate=SMALL,
    )(momentum, grad, where, basis)
    am, ap, new_momentum = lax.optimization_barrier((am, ap, new_momentum))
    top, bottom = send(am[: rows // 2], "u", 1), send(ap[rows // 2 :], "u", -1)
    s1 = jnp.concatenate([shard, am], axis=0)
    r1p, r1m = send(s1, "v", 1), send(s1, "v", -1)
    f32, bf16 = jnp.float32, jnp.bfloat16
    second = at((1, 0), (2, 0), (0, -1), (-1, -1), (0, 1), (-1, 1))
    third = at((1, -1), (2, -1), (1, 1), (2, 1))
    near, far = [(0, 2), (-1, 2)], [(1, 2), (2, 2)]
    fourth, fifth, sixth = at(*near), at(*near, other=True) + at(*far), at(*far, other=True)
    mine, theirs, *laid, ran = multiply(
        places,
        [(tokens, (), f32), (tokens_too, (), f32)],
        at((0, 0), (-1, 0)),
        [s1],
        ahead=[(tokens, second), (tokens_too, second)],
        flops=10**10,
    )
    top, bottom, ran = lax.optimization_barrier((top, bottom, ran))
    s2 = jnp.concatenate([ap, top, bottom], axis=0)
    r2p, r2m = send(s2, "v", 1), send(s2, "v", -1)
    f1 = send(r1p, "v", 1)
    mine, theirs, *laid, ran = multiply(
        places,
        [(laid[0], (mine,), f32), (laid[1], (theirs,), f32)],
        second,
        [s2, r1p, r1m],
        ran,
        ahead=[(tokens, third), (tokens_too, third)],
    )
    r2m, ran = lax.optimization_barrier((r2m, ran))
    f2 = send(r2m, "v", -1)
    mine, theirs, *laid, ran = multiply(
        places,
        [(laid[0], (mine,), f32), (laid[1], (theirs,), bf16)],
        third,
        [r2p, r2m],
        ran,
        ahead=[(tokens, some) for some in (fourth, fifth, sixth)],
    )
    theirs = sibling(theirs)
    f1, ran = lax.optimization_barrier((f1, ran))
    g1 = sibling(f1)
    mine, ran = multiply(places, [(laid[0], (mine,), f32)], fourth, [f1], ran)
    f2, ran = lax.optimization_barrier((f2, ran))
    g2 = sibling(f2)
    mine, ran = multiply(places, [(laid[1], (mine,), f32)], fifth, [g1, f2], ran)
    keys, _ = multiply(places, [(laid[2], (mine, theirs), bf16)], sixth, [g2], ran)
    return keys, shard, new_momentum


def solution(mesh):
    chips = Mesh(mesh.devices.reshape(REPS, SIDE, SIDE, 2), ("x",) + PLANE)
    return jax.shard_map(
        on_device,
        mesh=chips,
        in_specs=(
            P(("x",) + PLANE, None),
            P(PLANE, None),
            P("x", PLANE, None),
            P("x", PLANE, None),
            P(),
        ),
        out_specs=(P(("x",) + PLANE, None), P(PLANE, None), P("x", PLANE, None)),
        check_vma=False,
    )
```
